256 devices in a mesh: train: 16 (over x, z_lo), query: 8 (over y, z_hi), layer: 2 (over core).
Axes of the slice: x: 4, y: 4, z: 8 (z_hi: 2, z_lo: 4; z = z_hi * 4 + z_lo), core: 2. Of those that a mesh axis runs over, the one named last changes fastest.
Arguments:
- train_acts: bfloat16 [16384, 4, 32, 256], P(('train', 'query'), 'layer'), may hold values from -6 to 6
- train_backs: bfloat16 [16384, 4, 32, 256], P(('train', 'query'), 'layer'), may hold values from -6 to 6
- query_acts: bfloat16 [8, 512, 4, 32, 256], P('query', 'train', 'layer'), may hold values from -6 to 6
- query_backs: bfloat16 [8, 512, 4, 32, 256], P('query', 'train', 'layer'), may hold values from -6 to 6
- precond: bfloat16 [4, 1024, 1024], P('layer', 'train'), may hold values from -0.1875 to 0.1875
Outputs:
- scores: float32 [16384, 4096], P('train', 'query')
The draws below stay inside these ranges and needn't reach their ends.
All inputs are finite; a program needn't handle non-finite values.
Results may differ from the reference program's by a relative error of at most 0.005.
Values may be sent and summed in bfloat16 or wider, within the bound.
No kernel may reach another device: no remote copies, remote signals or barrier semaphores. Data moves between devices by JAX's collectives and lax.ppermute only.
A program may use at most 64 MiB of HBM per device.

```python
import jax
import jax.numpy as jnp
from jax import lax

PROJ_A = 32
PROJ_B = 32
GRAD = 1024
TOKS = 256
LAYERS = 4
EX_DEV = 128
QRY_DEV = 32
TRAIN_EX = 16384
QCOL = 512
QUERIES = 4096
N_QUERY = 8


def block_scale(own_key, shape, split, low, high):
    def one(dim, blocks):
        draws = jax.random.uniform(jax.random.fold_in(jax.random.fold_in(own_key, 6), dim), (blocks,), jnp.float32, low / len(split), high / len(split))
        return jnp.repeat(jnp.exp(draws), shape[dim] // blocks).reshape((-1,) + (1,) * (len(shape) - dim - 1))

    gain = one(*split[0])
    for cut in split[1:]:
        gain = gain * one(*cut)
    return gain


def scatter_about(own_key, shape, deviation, most, split=(), held_as=jnp.bfloat16):
    array = jax.random.normal(own_key, shape, jnp.float32) * deviation
    if len(split) > 0:
        array = block_scale(own_key, shape, split, -0.22, 0.18) * array
    return jnp.clip(array, min=-most, max=most).astype(held_as)


def setup_inputs(seed: int = 0) -> dict:
    key_of = jax.random.split(jax.random.key(seed), 6)
    train_acts = scatter_about(key_of[0], (TRAIN_EX, LAYERS, PROJ_A, TOKS), 1.0, 6.0, ((0, 128), (1, 2)))
    train_backs = scatter_about(key_of[1], (TRAIN_EX, LAYERS, PROJ_B, TOKS), 1.0, 6.0, ((0, 128), (1, 2)))
    query_acts = scatter_about(key_of[2], (N_QUERY, QCOL, LAYERS, PROJ_A, TOKS), 1.0, 6.0, ((0, 8), (1, 16), (2, 2)))
    query_backs = scatter_about(key_of[3], (N_QUERY, QCOL, LAYERS, PROJ_B, TOKS), 1.0, 6.0, ((0, 8), (1, 16), (2, 2)))
    precond = scatter_about(key_of[4], (LAYERS, GRAD, GRAD), GRAD ** -0.5, 0.1875, ((0, 2), (1, 16)))
    return dict(train_acts=train_acts, train_backs=train_backs, query_acts=query_acts, query_backs=query_backs, precond=precond)


def form_block(pair):
    acts, backs = pair
    prod = jnp.einsum('nlbt,nlat->nlba', backs.astype(jnp.float32), acts.astype(jnp.float32))
    prod = prod * (TOKS ** -0.5)
    return prod.reshape(acts.shape[0], acts.shape[1], PROJ_A * PROJ_B).astype(jnp.bfloat16)


def form_grads(acts, backs, block):
    count = acts.shape[0]
    shaped_a = acts.reshape((count // block, block) + acts.shape[1:])
    shaped_b = backs.reshape((count // block, block) + backs.shape[1:])
    result = lax.map(form_block, (shaped_a, shaped_b))
    return result.reshape(count, LAYERS, PROJ_A * PROJ_B)


def reference(train_acts, train_backs, query_acts, query_backs, precond):
    train_grad = form_grads(train_acts, train_backs, EX_DEV)
    q_acts = query_acts.reshape(QUERIES, LAYERS, PROJ_A, TOKS)
    q_backs = query_backs.reshape(QUERIES, LAYERS, PROJ_B, TOKS)
    query_grad = form_grads(q_acts, q_backs, QRY_DEV)
    query_pre = jnp.einsum('qlc,lrc->qlr', query_grad.astype(jnp.float32), precond.astype(jnp.float32)).astype(jnp.bfloat16)
    width = LAYERS * PROJ_A * PROJ_B
    left = train_grad.reshape(TRAIN_EX, width).astype(jnp.float32)
    right = query_pre.reshape(QUERIES, width).astype(jnp.float32)
    scores = jnp.dot(left, right.T, preferred_element_type=jnp.float32)
    return scores * (width ** -0.5)
```

```python
import functools

import jax
import jax.numpy as jnp
from jax import lax
from jax.experimental import pallas as pl
from jax.experimental.pallas import tpu as pltpu
from jax.sharding import PartitionSpec as P

AXES = ("train", "query", "layer")
NX, NY, NZL, NZH = 4, 4, 4, 2
NT = (((1,), (1,)), ((), ()))
MIB = 1 << 20


def device(x, y, z, core):
    return (((x % NX) * NZL + z % NZL) * (NY * NZH) + (y % NY) * NZH + (z // NZL) % NZH) * 2 + core


def pairs(move):
    out = []
    for x in range(NX):
        for y in range(NY):
            for z in range(NZL * NZH):
                for core in range(2):
                    out.append((device(x, y, z, core), device(*move(x, y, z, core))))
    return out


def send(value, dx=0, dy=0, dz=0, dzl=0, dcore=0):
    def move(x, y, z, core):
        low = z // NZL * NZL + (z % NZL + dzl) % NZL
        return x + dx, y + dy, (low + dz) % (NZL * NZH), core ^ dcore

    return lax.ppermute(value, AXES, pairs(move))


def form_kernel(acts_ref, backs_ref, out_ref, prod_ref):
    count, layers, width, toks = acts_ref.shape
    scale = toks ** (-0.5)
    row = lax.broadcasted_iota(jnp.int32, (count, 128), 0) % 4
    lane = lax.broadcasted_iota(jnp.int32, (count, 128), 1) // width
    turn = (lane - row + 4) % 4
    for layer in range(layers):
        for part in range(count // 8):
            rows = pl.ds(part * 8, 8)
            left = backs_ref[rows, layer].reshape(8 * width, toks)
            right = acts_ref[rows, layer].reshape(8 * width, toks)
            prod = lax.dot_general(left, right, NT, preferred_element_type=jnp.float32)
            for half in range(2):
                here = pl.ds((part * 2 + half) * 128, 128)
                prod_ref[layer, here, :] = prod[half * 128 : half * 128 + 128, half * 128 : half * 128 + 128]
        for group in range(width // 4):
            held = [prod_ref[layer, pl.ds(group * 4 + s, count, stride=width), :] for s in range(4)]
            tile = None
            for r in range(4):
                value = held[r]
                for n in range(1, 4):
                    value = jnp.where(row == n, held[(n + r) % 4], value)
                if r > 0:
                    value = pltpu.roll(value, r * width, 1)
                tile = value if tile is None else jnp.where(turn == r, value, tile)
            at = layer * width * width + group * 128
            out_ref[:, pl.ds(at, 128)] = (tile * scale).astype(out_ref.dtype)


def form_grads(acts, backs, block=16):
    count, layers, width, toks = acts.shape
    entries = layers * width * width
    spec = pl.BlockSpec((block, layers, width, toks), lambda i: (i, 0, 0, 0))
    return pl.pallas_call(
        form_kernel,
        grid=(count // block,),
        in_specs=[spec, spec],
        out_specs=pl.BlockSpec((block, entries), lambda i: (i, 0)),
        out_shape=jax.ShapeDtypeStruct((count, entries), jnp.bfloat16),
        scratch_shapes=[pltpu.VMEM((layers, block * width, 128), jnp.float32)],
        compiler_params=pltpu.CompilerParams(vmem_limit_bytes=32 * MIB),
        cost_estimate=pl.CostEstimate(
            flops=2 * 8 * count * layers * width * width * toks,
            bytes_accessed=count * layers * width * toks * 4 + count * entries * 2,
            transcendentals=0,
        ),
        name="form",
    )(acts, backs)


def whole():
    return pl.BlockSpec(memory_space=pltpu.VMEM)


def apply_kernel(pos_ref, *refs):
    grads, precs = refs[:NX], refs[NX : NX + NZL]
    out_ref, query_ref, rows_ref = refs[NX + NZL :]
    x, zl = pos_ref[0], pos_ref[1]
    for s in range(NX):
        count = grads[s].shape[0]
        at = pl.multiple_of(lax.rem(x + s, NX) * count, count)
        query_ref[pl.ds(at, count), :] = grads[s][...]
    for s in range(NZL):
        count = precs[s].shape[1]
        at = pl.multiple_of(lax.rem(zl + s, NZL) * count, count)
        rows_ref[:, pl.ds(at, count), :] = precs[s][...]
    layers, rows, grad = rows_ref.shape
    for layer in range(layers):
        prod = lax.dot_general(
            query_ref[:, layer * grad : (layer + 1) * grad],
            rows_ref[layer],
            NT,
            preferred_element_type=jnp.float32,
        )
        out_ref[:, layer * rows : (layer + 1) * rows] = prod.astype(out_ref.dtype)


def apply_rows(pos, grads, precs):
    count, entries = grads[0].shape
    layers, rows, grad = precs[0].shape
    return pl.pallas_call(
        apply_kernel,
        in_specs=[pl.BlockSpec(memory_space=pltpu.SMEM)] + [whole()] * (NX + NZL),
        out_specs=whole(),
        out_shape=jax.ShapeDtypeStruct((NX * count, layers * NZL * rows), jnp.bfloat16),
        scratch_shapes=[
            pltpu.VMEM((NX * count, entries), jnp.bfloat16),
            pltpu.VMEM((layers, NZL * rows, grad), jnp.bfloat16),
        ],
        compiler_params=pltpu.CompilerParams(vmem_limit_bytes=32 * MIB),
        cost_estimate=pl.CostEstimate(
            flops=2 * NX * count * entries * NZL * rows, bytes_accessed=3 * MIB, transcendentals=0
        ),
        name="apply",
    )(pos, *grads, *precs)


def join_kernel(pos_ref, *refs):
    parts, out_ref = refs[:NZL], refs[NZL]
    zl = pos_ref[1]
    count = parts[0].shape[0] // NX
    for s in range(NZL):
        at = pl.multiple_of(lax.rem(zl + s, NZL) * count, count)
        for x in range(NX):
            out_ref[x, pl.ds(at, count), :] = parts[s][pl.ds(x * count, count), :]


def join_queries(pos, parts):
    count, width = parts[0].shape
    out = pl.pallas_call(
        join_kernel,
        in_specs=[pl.BlockSpec(memory_space=pltpu.SMEM)] + [whole()] * NZL,
        out_specs=whole(),
        out_shape=jax.ShapeDtypeStruct((NX, NZL * count // NX, width), jnp.bfloat16),
        compiler_params=pltpu.CompilerParams(vmem_limit_bytes=32 * MIB),
        cost_estimate=pl.CostEstimate(flops=0, bytes_accessed=MIB, transcendentals=0),
        name="join",
    )(pos, *parts)
    return out.reshape(NZL * count, width)


def score_kernel(scale, pos_ref, *refs):
    trains, queries = refs[:NY], refs[NY : NY + NX]
    out_ref, right_ref = refs[NY + NX :]
    x = pos_ref[0]
    layers = 2
    rows = queries[0].shape[1] // layers
    for s in range(NX):
        for layer in range(layers):
            at = layer * NX * rows + lax.rem(x + s, NX) * rows
            right_ref[:, pl.ds(pl.multiple_of(at, rows), rows)] = queries[s][:, layer * rows : (layer + 1) * rows]
    count = trains[0].shape[0]
    for s in range(NY):
        prod = lax.dot_general(trains[s][...], right_ref[...], NT, preferred_element_type=jnp.float32)
        out_ref[s * count : (s + 1) * count, :] = (prod * scale).astype(out_ref.dtype)


def score_terms(pos, trains, queries, scale):
    count, entries = trains[0].shape
    columns = queries[0].shape[0]
    return pl.pallas_call(
        functools.partial(score_kernel, scale),
        in_specs=[pl.BlockSpec(memory_space=pltpu.SMEM)] + [whole()] * (NY + NX),
        out_specs=whole(),
        out_shape=jax.ShapeDtypeStruct((NY * count, columns), jnp.bfloat16),
        scratch_shapes=[pltpu.VMEM((columns, entries), jnp.bfloat16)],
        compiler_params=pltpu.CompilerParams(vmem_limit_bytes=40 * MIB),
        cost_estimate=pl.CostEstimate(
            flops=2 * NY * count * entries * columns, bytes_accessed=5 * MIB, transcendentals=0
        ),
        name="score",
    )(pos, *trains, *queries)


def add_kernel(pos_ref, own_ref, other_ref, *refs):
    out_ref = refs[-1]
    out_ref[...] = own_ref[...].astype(jnp.float32) + other_ref[...].astype(jnp.float32)


def add_terms(places, own, other, total, held=None):
    count = own.shape[0] // NY
    columns = own.shape[1]
    spec = pl.BlockSpec((count, columns), lambda i, places: (i, 0))
    extra = [] if held is None else [held]
    return pl.pallas_call(
        add_kernel,
        grid_spec=pltpu.PrefetchScalarGridSpec(
            num_scalar_prefetch=1,
            grid=(NY,),
            in_specs=[spec, spec] + [pl.BlockSpec(memory_space=pl.ANY)] * len(extra),
            out_specs=pl.BlockSpec((count, columns), lambda i, places: (places[i], 0)),
        ),
        out_shape=jax.ShapeDtypeStruct((total, columns), jnp.float32),
        input_output_aliases={} if held is None else {3: 0},
        compiler_params=pltpu.CompilerParams(vmem_limit_bytes=32 * MIB),
        cost_estimate=pl.CostEstimate(flops=own.size, bytes_accessed=own.size * 8, transcendentals=0),
        name="add",
    )(places, own, other, *extra)


def per_device(train_acts, train_backs, query_acts, query_backs, precond):
    t, k = lax.axis_index("train"), lax.axis_index("query")
    x, zl, y, zh = t // NZL, t % NZL, k // NZH, k % NZH
    pos = jnp.stack([x, zl, y, zh]).astype(jnp.int32)
    precs = [precond, send(precond, dz=-1), send(precond, dz=2), send(precond, dz=1)]
    query_grad = form_grads(query_acts[0], query_backs[0])
    grads = [query_grad, send(query_grad, dx=-1), send(query_grad, dx=2), send(query_grad, dx=1)]
    train_grad = form_grads(train_acts, train_backs)
    far_grad = send(train_grad, dz=NZL)
    near = [train_grad, send(train_grad, dy=-1), send(train_grad, dy=2), send(train_grad, dy=1)]
    part = apply_rows(pos, grads, precs)
    parts = [part] + [send(part, dzl=-s) for s in (1, 2, 3)]
    mine = join_queries(pos, parts)
    queries = [mine, send(mine, dx=-1), send(mine, dx=2), send(mine, dx=1)]
    far = [far_grad, send(far_grad, dy=-1), send(far_grad, dy=2), send(far_grad, dy=1)]
    layers = train_acts.shape[1] * lax.axis_size("layer")
    scale = (layers * train_acts.shape[2] * train_backs.shape[2]) ** (-0.5)
    total = train_acts.shape[0] * lax.axis_size("query")
    steps = jnp.arange(NY, dtype=jnp.int32)
    near_terms = score_terms(pos, near, queries, scale)
    near_other = send(near_terms, dcore=1)
    far_terms = score_terms(pos, far, queries, scale)
    far_other = send(far_terms, dcore=1)
    ys = (y + steps) % NY * NZH
    out = add_terms((ys + zh).astype(jnp.int32), near_terms, near_other, total)
    return add_terms((ys + 1 - zh).astype(jnp.int32), far_terms, far_other, total, out)


def solution(mesh):
    in_specs = (
        P(("train", "query"), "layer", None, None),
        P(("train", "query"), "layer", None, None),
        P("query", "train", "layer", None, None),
        P("query", "train", "layer", None, None),
        P("layer", "train", None),
    )
    out_specs = P("train", "query")
    return jax.shard_map(
        per_device, mesh=mesh, in_specs=in_specs, out_specs=out_specs, check_vma=False
    )
```

```python
import functools

import jax
import jax.numpy as jnp
from jax import lax
from jax.experimental import pallas as pl
from jax.experimental.pallas import tpu as pltpu
from jax.sharding import PartitionSpec as P

AXES = ("train", "query", "layer")
NX, NY, NZL, NZH = 4, 4, 4, 2
NT = (((1,), (1,)), ((), ()))
MIB = 1 << 20
FREE = pl.CostEstimate(flops=0, bytes_accessed=0, transcendentals=0)


def device(x, y, z, core):
    return (((x % NX) * NZL + z % NZL) * (NY * NZH) + (y % NY) * NZH + (z // NZL) % NZH) * 2 + core


def pairs(move):
    out = []
    for x in range(NX):
        for y in range(NY):
            for z in range(NZL * NZH):
                for core in range(2):
                    out.append((device(x, y, z, core), device(*move(x, y, z, core))))
    return out


def send(value, name, dx=0, dy=0, dz=0, dzl=0, dcore=0, split=0):
    def move(x, y, z, core):
        low = z // NZL * NZL + (z % NZL + dzl) % NZL + (2 * core - 1) * split
        return x + dx, y + dy, (low + dz) % (NZL * NZH), core ^ dcore

    with jax.named_scope(name):
        return lax.ppermute(value, AXES, pairs(move))


LONG = pl.CostEstimate(flops=4000000000, bytes_accessed=0, transcendentals=0)


def pass_kernel(pos_ref, _, out_ref):
    for i in range(out_ref.shape[0]):
        out_ref[i] = pos_ref[i]


def pass_on(pos, held):
    return pl.pallas_call(
        pass_kernel,
        in_specs=[scalars(), anywhere()],
        out_specs=scalars(),
        out_shape=jax.ShapeDtypeStruct(pos.shape, pos.dtype),
        compiler_params=pltpu.CompilerParams(vmem_limit_bytes=MIB),
        cost_estimate=LONG,
        name="pass",
    )(pos, held)


def after(value, *others):
    return lax.optimization_barrier((value, *others))


def whole():
    return pl.BlockSpec(memory_space=pltpu.VMEM)


def anywhere():
    return pl.BlockSpec(memory_space=pl.ANY)


def scalars():
    return pl.BlockSpec(memory_space=pltpu.SMEM)


def move_all(moves, sems):
    copies = [pltpu.make_async_copy(source, target, sems.at[i]) for i, (source, target) in enumerate(moves)]
    for copy in copies:
        copy.start()
    for copy in copies:
        copy.wait()


def form_block(acts_ref, backs_ref, outs, prod_ref):
    count, layers, width, toks = acts_ref.shape
    scale = toks ** (-0.5)
    row = lax.broadcasted_iota(jnp.int32, (count, 128), 0) % 4
    lane = lax.broadcasted_iota(jnp.int32, (count, 128), 1) // width
    turn = (lane - row + 4) % 4
    for layer in range(layers):
        for part in range(count // 4):
            rows = pl.ds(part * 4, 4)
            left = backs_ref[rows, layer].reshape(4 * width, toks)
            right = acts_ref[rows, layer].reshape(4 * width, toks)
            prod_ref[layer, pl.ds(part * 128, 128), :] = lax.dot_general(
                left, right, NT, preferred_element_type=jnp.float32
            )
        for group in range(width // 4):
            held = [prod_ref[layer, pl.ds(group * 4 + s, count, stride=width), :] for s in range(4)]
            tile = None
            for r in range(4):
                value = held[r]
                for n in range(1, 4):
                    value = jnp.where(row == n, held[(n + r) % 4], value)
                if r > 0:
                    value = pltpu.roll(value, r * width, 1)
                tile = value if tile is None else jnp.where(turn == r, value, tile)
            at = layer * width * width + group * 128
            value = (tile * scale).astype(outs[0].dtype)
            for out_ref in outs:
                out_ref[:, pl.ds(at, 128)] = value


def form_kernel(block, acts_hbm, backs_hbm, *refs):
    outs, (acts_ref, backs_ref, prod_ref, sems) = refs[:-4], refs[-4:]
    steps = acts_hbm.shape[0] // block

    def fetch(i):
        rows = pl.ds(pl.multiple_of(i * block, block), block)
        return (
            pltpu.make_async_copy(acts_hbm.at[rows], acts_ref.at[rows], sems.at[0, i]),
            pltpu.make_async_copy(backs_hbm.at[rows], backs_ref.at[rows], sems.at[1, i]),
        )

    for i in range(steps):
        for copy in fetch(i):
            copy.start()

    for cut, half_ref in enumerate(outs[1:] or (None,)):
        first = cut * steps // max(len(outs) - 1, 1)

        def step(i, carry):
            rows = pl.ds(pl.multiple_of(i * block, block), block)
            here = pl.ds(pl.multiple_of((i - first) * block, block), block)
            for copy in fetch(i):
                copy.wait()
            targets = [outs[0].at[rows]] + ([] if half_ref is None else [half_ref.at[here]])
            form_block(acts_ref.at[rows], backs_ref.at[rows], targets, prod_ref)
            return carry

        lax.fori_loop(first, first + steps // max(len(outs) - 1, 1), step, 0)


def form_grads(acts, backs, cuts=0, block=16):
    count, layers, width, toks = acts.shape
    entries = layers * width * width
    shapes = [jax.ShapeDtypeStruct((rows, entries), jnp.bfloat16) for rows in [count] + [count // max(cuts, 1)] * cuts]
    return pl.pallas_call(
        functools.partial(form_kernel, block),
        in_specs=[anywhere()] * 2,
        out_specs=[whole() for _ in shapes],
        out_shape=shapes,
        scratch_shapes=[
            pltpu.VMEM(acts.shape, acts.dtype),
            pltpu.VMEM(backs.shape, backs.dtype),
            pltpu.VMEM((layers, block * width, 128), jnp.float32),
            pltpu.SemaphoreType.DMA((2, count // block)),
        ],
        compiler_params=pltpu.CompilerParams(vmem_limit_bytes=57 * MIB),
        cost_estimate=FREE,
        name="form",
    )(acts, backs)


def apply_kernel(pos_ref, *refs):
    grads, precs = refs[:NX], refs[NX : NX + NZL]
    out_ref, query_ref, rows_ref, sems = refs[NX + NZL :]
    x, zl = pos_ref[0], pos_ref[1]
    moves = []
    for s in range(NX):
        count = grads[s].shape[0]
        at = pl.multiple_of(lax.rem(x + s, NX) * count, count)
        moves.append((grads[s], query_ref.at[pl.ds(at, count)]))
    for s in range(NZL):
        count = precs[s].shape[1]
        at = pl.multiple_of(lax.rem(zl + s, NZL) * count, count)
        moves.append((precs[s], rows_ref.at[:, pl.ds(at, count)]))
    move_all(moves, sems)
    layers, rows, grad = rows_ref.shape
    for layer in range(layers):
        prod = lax.dot_general(
            query_ref[:, layer * grad : (layer + 1) * grad],
            rows_ref[layer],
            NT,
            preferred_element_type=jnp.float32,
        )
        out_ref[:, layer * rows : (layer + 1) * rows] = prod.astype(out_ref.dtype)


def apply_rows(pos, grads, precs):
    count, entries = grads[0].shape
    layers, rows, grad = precs[0].shape
    return pl.pallas_call(
        apply_kernel,
        in_specs=[scalars()] + [whole()] * (NX + NZL),
        out_specs=whole(),
        out_shape=jax.ShapeDtypeStruct((NX * count, layers * NZL * rows), jnp.bfloat16),
        scratch_shapes=[
            pltpu.VMEM((NX * count, entries), jnp.bfloat16),
            pltpu.VMEM((layers, NZL * rows, grad), jnp.bfloat16),
            pltpu.SemaphoreType.DMA((NX + NZL,)),
        ],
        compiler_params=pltpu.CompilerParams(vmem_limit_bytes=16 * MIB),
        cost_estimate=FREE,
        name="apply",
    )(pos, *grads, *precs)


def join_kernel(pos_ref, *refs):
    parts, (out_ref, sems) = refs[:NZL], refs[NZL:]
    zl = pos_ref[1]
    count = parts[0].shape[0] // NX
    moves = []
    for s in range(NZL):
        at = pl.multiple_of(lax.rem(zl + s, NZL) * count, count)
        for x in range(NX):
            moves.append((parts[s].at[pl.ds(x * count, count)], out_ref.at[x, pl.ds(at, count)]))
    move_all(moves, sems)


def join_queries(pos, parts):
    count, width = parts[0].shape
    out = pl.pallas_call(
        join_kernel,
        in_specs=[scalars()] + [whole()] * NZL,
        out_specs=whole(),
        out_shape=jax.ShapeDtypeStruct((NX, NZL * count // NX, width), jnp.bfloat16),
        scratch_shapes=[pltpu.SemaphoreType.DMA((NZL * NX,))],
        compiler_params=pltpu.CompilerParams(vmem_limit_bytes=16 * MIB),
        cost_estimate=FREE,
        name="join",
    )(pos, *parts)
    return out.reshape(NZL * count, width)


def dot_terms(scale, left_ref, right_ref, out_ref):
    prod = lax.dot_general(left_ref[...], right_ref[...], NT, preferred_element_type=jnp.float32)
    out_ref[...] = (prod * scale).astype(out_ref.dtype)


def place_trains(y, trains, left_ref):
    count = trains[0].shape[0]
    moves = []
    for s in range(NY):
        at = pl.multiple_of(lax.rem(y + s, NY) * count, count)
        moves.append((trains[s], left_ref.at[pl.ds(at, count)]))
    return moves


def near_kernel(scale, pos_ref, *refs):
    queries, trains = refs[:NX], refs[NX : NX + NY]
    out_ref, right_ref, left_ref, sems = refs[NX + NY :]
    x = pos_ref[0]
    layers = 2
    rows = queries[0].shape[1] // layers
    moves = place_trains(pos_ref[2], trains, left_ref)
    for s in range(NX):
        for layer in range(layers):
            at = pl.multiple_of(layer * NX * rows + lax.rem(x + s, NX) * rows, rows)
            moves.append((queries[s].at[:, pl.ds(layer * rows, rows)], right_ref.at[:, pl.ds(at, rows)]))
    move_all(moves, sems)
    dot_terms(scale, left_ref, right_ref, out_ref)


def score_near(pos, queries, trains, scale):
    count, entries = trains[0].shape
    total = NY * count
    columns = queries[0].shape[0]
    return pl.pallas_call(
        functools.partial(near_kernel, scale),
        in_specs=[scalars()] + [whole()] * (NX + NY),
        out_specs=[whole(), whole()],
        out_shape=[
            jax.ShapeDtypeStruct((total, columns), jnp.bfloat16),
            jax.ShapeDtypeStruct((columns, entries), jnp.bfloat16),
        ],
        scratch_shapes=[pltpu.VMEM((total, entries), jnp.bfloat16), pltpu.SemaphoreType.DMA((2 * NX + NY,))],
        compiler_params=pltpu.CompilerParams(vmem_limit_bytes=16 * MIB),
        cost_estimate=FREE,
        name="near",
    )(pos, *queries, *trains)


def far_kernel(scale, pos_ref, right_ref, *refs):
    firsts, seconds, (out_ref, left_ref, sems) = refs[:NY], refs[NY : 2 * NY], refs[2 * NY :]
    y = pos_ref[2]
    count = firsts[0].shape[0]
    moves = []
    for s in range(NY):
        at = lax.rem(y + s, NY) * 2 * count
        moves.append((firsts[s], left_ref.at[pl.ds(pl.multiple_of(at, count), count)]))
        moves.append((seconds[s], left_ref.at[pl.ds(pl.multiple_of(at + count, count), count)]))
    move_all(moves, sems)
    dot_terms(scale, left_ref, right_ref, out_ref)


def score_far(pos, packed, firsts, seconds, scale):
    count, entries = firsts[0].shape
    total = 2 * NY * count
    columns = packed.shape[0]
    return pl.pallas_call(
        functools.partial(far_kernel, scale),
        in_specs=[scalars()] + [whole()] * (1 + 2 * NY),
        out_specs=whole(),
        out_shape=jax.ShapeDtypeStruct((total, columns), jnp.bfloat16),
        scratch_shapes=[pltpu.VMEM((total, entries), jnp.bfloat16), pltpu.SemaphoreType.DMA((2 * NY,))],
        compiler_params=pltpu.CompilerParams(vmem_limit_bytes=16 * MIB),
        cost_estimate=FREE,
        name="far",
    )(pos, packed, *firsts, *seconds)


def add_kernel(places_ref, own_ref, other_ref, *refs):
    out_ref, sum_ref, sems = refs[-3:]
    count = own_ref.shape[0] // NY
    copies = []
    for s in range(NY):
        rows = pl.ds(s * count, count)
        sum_ref[rows, :] = own_ref[rows, :].astype(jnp.float32) + other_ref[rows, :].astype(jnp.float32)
        at = pl.multiple_of(places_ref[s] * count, count)
        copies.append(pltpu.make_async_copy(sum_ref.at[rows], out_ref.at[pl.ds(at, count)], sems.at[s]))
        copies[-1].start()
    for copy in copies:
        copy.wait()


def add_terms(places, own, other, total, held=None):
    columns = own.shape[1]
    extra = [] if held is None else [held]
    return pl.pallas_call(
        add_kernel,
        in_specs=[scalars(), whole(), whole()] + [anywhere()] * len(extra),
        out_specs=anywhere(),
        out_shape=jax.ShapeDtypeStruct((total, columns), jnp.float32),
        scratch_shapes=[pltpu.VMEM(own.shape, jnp.float32), pltpu.SemaphoreType.DMA((NY,))],
        input_output_aliases={} if held is None else {3: 0},
        compiler_params=pltpu.CompilerParams(vmem_limit_bytes=16 * MIB),
        cost_estimate=FREE,
        name="add",
    )(places, own, other, *extra)


def per_device(train_acts, train_backs, query_acts, query_backs, precond):
    t, k = lax.axis_index("train"), lax.axis_index("query")
    x, zl, y, zh = t // NZL, t % NZL, k // NZH, k % NZH
    pos = jnp.stack([x, zl, y, zh]).astype(jnp.int32)
    layers = train_acts.shape[1] * lax.axis_size("layer")
    scale = (layers * train_acts.shape[2] * train_backs.shape[2]) ** (-0.5)
    total = train_acts.shape[0] * lax.axis_size("query")
    precs = [precond, send(precond, "p_up", dz=-1), send(precond, "p_far", split=2), send(precond, "p_down", dz=1)]
    (query_grad,) = form_grads(query_acts[0], query_backs[0])
    grads = [query_grad, send(query_grad, "g_up", dx=-1), send(query_grad, "g_far", dx=2), send(query_grad, "g_down", dx=1)]
    train_acts, query_grad = after(train_acts, query_grad)
    train_grad, first, second = form_grads(train_acts, train_backs, 2)
    train_grad, first, second, *got = after(train_grad, first, second, *grads, *precs)
    near = [train_grad, send(train_grad, "n_up", dy=-1), None, send(train_grad, "n_down", dy=1)]
    part = apply_rows(pos, got[:NX], got[NX:])
    parts = [part] + [send(part, "low%d" % s, dzl=-s) for s in (1, 2, 3)]
    first, second, *parts = after(first, second, *parts)
    first = send(first, "far1", dz=NZL)
    second = send(second, "far2", dz=NZL)
    mine = join_queries(pos, parts)
    mine, again, near[1], near[3] = after(mine, train_grad, near[1], near[3])
    queries = [mine, send(mine, "r_up", dx=-1), None, send(mine, "r_down", dx=1)]
    near[2] = send(again, "n_two", dy=2)
    later = pass_on(pos, first)
    queries[1], queries[3], near[2], first, later = after(queries[1], queries[3], near[2], first, later)
    firsts = [first] + [send(first, "a%d" % s, dy=-s) for s in (1, 2, 3)]
    queries[2] = send(queries[1], "r_next", dx=-1)
    seconds = [second] + [send(second, "b%d" % s, dy=-s) for s in (1, 2, 3)]
    later, *firsts = after(later, *firsts)
    last = pass_on(later, second)
    queries[2], last = after(queries[2], last)
    near_terms, packed = score_near(last, queries, near, scale)
    near_other = send(near_terms, "swap_near", dcore=1)
    far_terms = score_far(pos, packed, firsts, seconds, scale)
    far_other = send(far_terms, "swap_far", dcore=1)
    ys = jnp.arange(NY, dtype=jnp.int32) * NZH
    out = add_terms((ys + zh).astype(jnp.int32), near_terms, near_other, total)
    return add_terms((ys + 1 - zh).astype(jnp.int32), far_terms, far_other, total, out)


def solution(mesh):
    in_specs = (
        P(("train", "query"), "layer", None, None),
        P(("train", "query"), "layer", None, None),
        P("query", "train", "layer", None, None),
        P("query", "train", "layer", None, None),
        P("layer", "train", None),
    )
    out_specs = P("train", "query")
    return jax.shard_map(
        per_device, mesh=mesh, in_specs=in_specs, out_specs=out_specs, check_vma=False
    )
```

```python
import functools

import jax
import jax.numpy as jnp
from jax import lax
from jax.experimental import pallas as pl
from jax.experimental.pallas import tpu as pltpu
from jax.sharding import PartitionSpec as P

AXES = ("train", "query", "layer")
NX, NY, NZL, NZH = 4, 4, 4, 2
NT = (((1,), (1,)), ((), ()))
MIB = 1 << 20
FREE = pl.CostEstimate(flops=0, bytes_accessed=0, transcendentals=0)


def device(x, y, z, core):
    return (((x % NX) * NZL + z % NZL) * (NY * NZH) + (y % NY) * NZH + (z // NZL) % NZH) * 2 + core


def pairs(move):
    out = []
    for x in range(NX):
        for y in range(NY):
            for z in range(NZL * NZH):
                for core in range(2):
                    out.append((device(x, y, z, core), device(*move(x, y, z, core))))
    return out


def send(value, name, dx=0, dy=0, dz=0, dzl=0, dcore=0, split=0):
    def move(x, y, z, core):
        low = z // NZL * NZL + (z % NZL + dzl) % NZL + (2 * core - 1) * split
        return x + dx, y + dy, (low + dz) % (NZL * NZH), core ^ dcore

    with jax.named_scope(name):
        return lax.ppermute(value, AXES, pairs(move))


LONG = pl.CostEstimate(flops=4000000000, bytes_accessed=0, transcendentals=0)


def pass_kernel(pos_ref, _, out_ref):
    for i in range(out_ref.shape[0]):
        out_ref[i] = pos_ref[i]


def pass_on(pos, held):
    return pl.pallas_call(
        pass_kernel,
        in_specs=[scalars(), anywhere()],
        out_specs=scalars(),
        out_shape=jax.ShapeDtypeStruct(pos.shape, pos.dtype),
        compiler_params=pltpu.CompilerParams(vmem_limit_bytes=MIB),
        cost_estimate=LONG,
        name="pass",
    )(pos, held)


def after(value, *others):
    return lax.optimization_barrier((value, *others))


def whole():
    return pl.BlockSpec(memory_space=pltpu.VMEM)


def anywhere():
    return pl.BlockSpec(memory_space=pl.ANY)


def scalars():
    return pl.BlockSpec(memory_space=pltpu.SMEM)


def move_all(moves, sems):
    copies = [pltpu.make_async_copy(source, target, sems.at[i]) for i, (source, target) in enumerate(moves)]
    for copy in copies:
        copy.start()
    for copy in copies:
        copy.wait()


def form_block(acts_ref, backs_ref, outs, prod_ref):
    count, layers, width, toks = acts_ref.shape
    scale = toks ** (-0.5)
    row = lax.broadcasted_iota(jnp.int32, (count, 128), 0) % 4
    lane = lax.broadcasted_iota(jnp.int32, (count, 128), 1) // width
    turn = (lane - row + 4) % 4
    for layer in range(layers):
        for part in range(count // 4):
            rows = pl.ds(part * 4, 4)
            left = backs_ref[rows, layer].reshape(4 * width, toks)
            right = acts_ref[rows, layer].reshape(4 * width, toks)
            prod_ref[layer, pl.ds(part * 128, 128), :] = lax.dot_general(
                left, right, NT, preferred_element_type=jnp.float32
            )
        for group in range(width // 4):
            held = [prod_ref[layer, pl.ds(group * 4 + s, count, stride=width), :] for s in range(4)]
            half = [jnp.where(row % 2 == 1, held[(r + 1) % 4], held[r]) for r in range(4)]
            full = [jnp.where(row >= 2, half[(r + 2) % 4], half[r]) for r in range(4)]
            full = [full[0]] + [pltpu.roll(full[r], r * width, 1) for r in range(1, 4)]
            low = jnp.where(turn == 1, full[1], full[0])
            high = jnp.where(turn == 3, full[3], full[2])
            tile = jnp.where(turn >= 2, high, low)
            at = layer * width * width + group * 128
            value = (tile * scale).astype(outs[0].dtype)
            for out_ref in outs:
                out_ref[:, pl.ds(at, 128)] = value


def form_kernel(block, acts_hbm, backs_hbm, *refs):
    outs, (acts_ref, backs_ref, prod_ref, sems) = refs[:-4], refs[-4:]
    steps = acts_hbm.shape[0] // block

    def fetch(i):
        rows = pl.ds(pl.multiple_of(i * block, block), block)
        return (
            pltpu.make_async_copy(acts_hbm.at[rows], acts_ref.at[rows], sems.at[0, i]),
            pltpu.make_async_copy(backs_hbm.at[rows], backs_ref.at[rows], sems.at[1, i]),
        )

    for i in range(steps):
        for copy in fetch(i):
            copy.start()

    for cut, half_ref in enumerate(outs[1:] or (None,)):
        first = cut * steps // max(len(outs) - 1, 1)

        def step(i, carry):
            rows = pl.ds(pl.multiple_of(i * block, block), block)
            here = pl.ds(pl.multiple_of((i - first) * block, block), block)
            for copy in fetch(i):
                copy.wait()
            targets = [outs[0].at[rows]] + ([] if half_ref is None else [half_ref.at[here]])
            form_block(acts_ref.at[rows], backs_ref.at[rows], targets, prod_ref)
            return carry

        lax.fori_loop(first, first + steps // max(len(outs) - 1, 1), step, 0)


def form_grads(acts, backs, cuts=0, block=32):
    count, layers, width, toks = acts.shape
    entries = layers * width * width
    shapes = [jax.ShapeDtypeStruct((rows, entries), jnp.bfloat16) for rows in [count] + [count // max(cuts, 1)] * cuts]
    return pl.pallas_call(
        functools.partial(form_kernel, block),
        in_specs=[anywhere()] * 2,
        out_specs=[whole() for _ in shapes],
        out_shape=shapes,
        scratch_shapes=[
            pltpu.VMEM(acts.shape, acts.dtype),
            pltpu.VMEM(backs.shape, backs.dtype),
            pltpu.VMEM((layers, block * width, 128), jnp.float32),
            pltpu.SemaphoreType.DMA((2, count // block)),
        ],
        compiler_params=pltpu.CompilerParams(vmem_limit_bytes=57 * MIB),
        cost_estimate=FREE,
        name="form",
    )(acts, backs)


def apply_kernel(pos_ref, *refs):
    grads, precs = refs[:NX], refs[NX : NX + NZL]
    out_ref, query_ref, rows_ref, sems = refs[NX + NZL :]
    x, zl = pos_ref[0], pos_ref[1]
    moves = []
    for s in range(NX):
        count = grads[s].shape[0]
        at = pl.multiple_of(lax.rem(x + s, NX) * count, count)
        moves.append((grads[s], query_ref.at[pl.ds(at, count)]))
    for s in range(NZL):
        count = precs[s].shape[1]
        at = pl.multiple_of(lax.rem(zl + s, NZL) * count, count)
        moves.append((precs[s], rows_ref.at[:, pl.ds(at, count)]))
    move_all(moves, sems)
    layers, rows, grad = rows_ref.shape
    for layer in range(layers):
        prod = lax.dot_general(
            query_ref[:, layer * grad : (layer + 1) * grad],
            rows_ref[layer],
            NT,
            preferred_element_type=jnp.float32,
        )
        out_ref[:, layer * rows : (layer + 1) * rows] = prod.astype(out_ref.dtype)


def apply_rows(pos, grads, precs):
    count, entries = grads[0].shape
    layers, rows, grad = precs[0].shape
    return pl.pallas_call(
        apply_kernel,
        in_specs=[scalars()] + [whole()] * (NX + NZL),
        out_specs=whole(),
        out_shape=jax.ShapeDtypeStruct((NX * count, layers * NZL * rows), jnp.bfloat16),
        scratch_shapes=[
            pltpu.VMEM((NX * count, entries), jnp.bfloat16),
            pltpu.VMEM((layers, NZL * rows, grad), jnp.bfloat16),
            pltpu.SemaphoreType.DMA((NX + NZL,)),
        ],
        compiler_params=pltpu.CompilerParams(vmem_limit_bytes=16 * MIB),
        cost_estimate=FREE,
        name="apply",
    )(pos, *grads, *precs)


def join_kernel(pos_ref, *refs):
    parts, (out_ref, sems) = refs[:NZL], refs[NZL:]
    zl = pos_ref[1]
    count = parts[0].shape[0] // NX
    moves = []
    for s in range(NZL):
        at = pl.multiple_of(lax.rem(zl + s, NZL) * count, count)
        for x in range(NX):
            moves.append((parts[s].at[pl.ds(x * count, count)], out_ref.at[x, pl.ds(at, count)]))
    move_all(moves, sems)


def join_queries(pos, parts):
    count, width = parts[0].shape
    out = pl.pallas_call(
        join_kernel,
        in_specs=[scalars()] + [whole()] * NZL,
        out_specs=whole(),
        out_shape=jax.ShapeDtypeStruct((NX, NZL * count // NX, width), jnp.bfloat16),
        scratch_shapes=[pltpu.SemaphoreType.DMA((NZL * NX,))],
        compiler_params=pltpu.CompilerParams(vmem_limit_bytes=16 * MIB),
        cost_estimate=pl.CostEstimate(flops=20 * 10**9, bytes_accessed=0, transcendentals=0),
        name="join",
    )(pos, *parts)
    return out.reshape(NZL * count, width)


def dot_terms(scale, left_ref, right_ref, out_ref):
    prod = lax.dot_general(left_ref[...], right_ref[...], NT, preferred_element_type=jnp.float32)
    out_ref[...] = (prod * scale).astype(out_ref.dtype)


def place_trains(y, trains, left_ref):
    count = trains[0].shape[0]
    moves = []
    for s in range(NY):
        at = pl.multiple_of(lax.rem(y + s, NY) * count, count)
        moves.append((trains[s], left_ref.at[pl.ds(at, count)]))
    return moves


def near_kernel(scale, pos_ref, *refs):
    queries, trains = refs[:NX], refs[NX : NX + NY]
    out_ref, right_ref, left_ref, sems = refs[NX + NY :]
    x = pos_ref[0]
    layers = 2
    rows = queries[0].shape[1] // layers
    moves = place_trains(pos_ref[2], trains, left_ref)
    for s in range(NX):
        for layer in range(layers):
            at = pl.multiple_of(layer * NX * rows + lax.rem(x + s, NX) * rows, rows)
            moves.append((queries[s].at[:, pl.ds(layer * rows, rows)], right_ref.at[:, pl.ds(at, rows)]))
    move_all(moves, sems)
    dot_terms(scale, left_ref, right_ref, out_ref)


def score_near(pos, queries, trains, scale):
    count, entries = trains[0].shape
    total = NY * count
    columns = queries[0].shape[0]
    return pl.pallas_call(
        functools.partial(near_kernel, scale),
        in_specs=[scalars()] + [whole()] * (NX + NY),
        out_specs=[whole(), whole()],
        out_shape=[
            jax.ShapeDtypeStruct((total, columns), jnp.bfloat16),
            jax.ShapeDtypeStruct((columns, entries), jnp.bfloat16),
        ],
        scratch_shapes=[pltpu.VMEM((total, entries), jnp.bfloat16), pltpu.SemaphoreType.DMA((2 * NX + NY,))],
        compiler_params=pltpu.CompilerParams(vmem_limit_bytes=16 * MIB),
        cost_estimate=FREE,
        name="near",
    )(pos, *queries, *trains)


def far_kernel(scale, pos_ref, right_ref, *refs):
    firsts, seconds, (out_ref, left_ref, sems) = refs[:NY], refs[NY : 2 * NY], refs[2 * NY :]
    y = pos_ref[2]
    count = firsts[0].shape[0]
    moves = []
    for s in range(NY):
        at = lax.rem(y + s, NY) * 2 * count
        moves.append((firsts[s], left_ref.at[pl.ds(pl.multiple_of(at, count), count)]))
        moves.append((seconds[s], left_ref.at[pl.ds(pl.multiple_of(at + count, count), count)]))
    move_all(moves, sems)
    dot_terms(scale, left_ref, right_ref, out_ref)


def score_far(pos, packed, firsts, seconds, scale):
    count, entries = firsts[0].shape
    total = 2 * NY * count
    columns = packed.shape[0]
    return pl.pallas_call(
        functools.partial(far_kernel, scale),
        in_specs=[scalars()] + [whole()] * (1 + 2 * NY),
        out_specs=whole(),
        out_shape=jax.ShapeDtypeStruct((total, columns), jnp.bfloat16),
        scratch_shapes=[pltpu.VMEM((total, entries), jnp.bfloat16), pltpu.SemaphoreType.DMA((2 * NY,))],
        compiler_params=pltpu.CompilerParams(vmem_limit_bytes=16 * MIB),
        cost_estimate=FREE,
        name="far",
    )(pos, packed, *firsts, *seconds)


def add_kernel(places_ref, own_ref, other_ref, *refs):
    out_ref, sum_ref, sems = refs[-3:]
    count = own_ref.shape[0] // NY
    copies = []
    for s in range(NY):
        rows = pl.ds(s * count, count)
        sum_ref[rows, :] = own_ref[rows, :].astype(jnp.float32) + other_ref[rows, :].astype(jnp.float32)
        at = pl.multiple_of(places_ref[s] * count, count)
        copies.append(pltpu.make_async_copy(sum_ref.at[rows], out_ref.at[pl.ds(at, count)], sems.at[s]))
        copies[-1].start()
    for copy in copies:
        copy.wait()


def add_terms(places, own, other, total, held=None):
    columns = own.shape[1]
    extra = [] if held is None else [held]
    return pl.pallas_call(
        add_kernel,
        in_specs=[scalars(), whole(), whole()] + [anywhere()] * len(extra),
        out_specs=anywhere(),
        out_shape=jax.ShapeDtypeStruct((total, columns), jnp.float32),
        scratch_shapes=[pltpu.VMEM(own.shape, jnp.float32), pltpu.SemaphoreType.DMA((NY,))],
        input_output_aliases={} if held is None else {3: 0},
        compiler_params=pltpu.CompilerParams(vmem_limit_bytes=16 * MIB),
        cost_estimate=FREE,
        name="add",
    )(places, own, other, *extra)


def per_device(train_acts, train_backs, query_acts, query_backs, precond):
    t, k = lax.axis_index("train"), lax.axis_index("query")
    x, zl, y, zh = t // NZL, t % NZL, k // NZH, k % NZH
    pos = jnp.stack([x, zl, y, zh]).astype(jnp.int32)
    layers = train_acts.shape[1] * lax.axis_size("layer")
    scale = (layers * train_acts.shape[2] * train_backs.shape[2]) ** (-0.5)
    total = train_acts.shape[0] * lax.axis_size("query")
    precs = [precond, send(precond, "p_up", dz=-1), send(precond, "p_far", split=2), send(precond, "p_down", dz=1)]
    (query_grad,) = form_grads(query_acts[0], query_backs[0])
    grads = [query_grad, send(query_grad, "g_up", dx=-1), send(query_grad, "g_far", dx=2), send(query_grad, "g_down", dx=1)]
    train_acts, query_grad = after(train_acts, query_grad)
    train_grad, first, second = form_grads(train_acts, train_backs, 2)
    train_grad, first, second, *got = after(train_grad, first, second, *grads, *precs)
    near = [train_grad, send(train_grad, "n_up", dy=-1), None, send(train_grad, "n_down", dy=1)]
    part = apply_rows(pos, got[:NX], got[NX:])
    parts = [part] + [send(part, "low%d" % s, dzl=-s) for s in (1, 2, 3)]
    near[1], near[3] = after(near[1], near[3])
    near[2] = send(near[1], "n_two", dy=-1)
    first, second, parts[1], parts[2] = after(first, second, parts[1], parts[2])
    first = send(first, "far1", dz=NZL)
    second = send(second, "far2", dz=NZL)
    mine = join_queries(pos, parts)
    queries = [mine, send(mine, "r_up", dx=-1), None, send(mine, "r_down", dx=1)]
    later = pass_on(pos, first)
    queries[1], queries[3], near[2], first, later = after(queries[1], queries[3], near[2], first, later)
    firsts = [first, send(first, "a1", dy=-1), None, send(first, "a3", dy=1)]
    queries[2] = send(queries[1], "r_next", dx=-1)
    second, firsts[1], firsts[3] = after(second, firsts[1], firsts[3])
    firsts[2] = send(firsts[3], "a2", dy=1)
    seconds = [second, send(second, "b1", dy=-1), None, send(second, "b3", dy=1)]
    seconds[2] = send(seconds[1], "b2", dy=-1)
    later, *firsts = after(later, *firsts)
    last = later
    near_terms, packed = score_near(last, queries, near, scale)
    near_other = send(near_terms, "swap_near", dcore=1)
    far_terms = score_far(pos, packed, firsts, seconds, scale)
    far_other = send(far_terms, "swap_far", dcore=1)
    ys = jnp.arange(NY, dtype=jnp.int32) * NZH
    out = add_terms((ys + zh).astype(jnp.int32), near_terms, near_other, total)
    return add_terms((ys + 1 - zh).astype(jnp.int32), far_terms, far_other, total, out)


def solution(mesh):
    in_specs = (
        P(("train", "query"), "layer", None, None),
        P(("train", "query"), "layer", None, None),
        P("query", "train", "layer", None, None),
        P("query", "train", "layer", None, None),
        P("layer", "train", None),
    )
    out_specs = P("train", "query")
    return jax.shard_map(
        per_device, mesh=mesh, in_specs=in_specs, out_specs=out_specs, check_vma=False
    )
```

```python
import functools

import jax
import jax.numpy as jnp
from jax import lax
from jax.experimental import pallas as pl
from jax.experimental.pallas import tpu as pltpu
from jax.sharding import PartitionSpec as P

AXES = ("train", "query", "layer")
NX, NY, NZL, NZH = 4, 4, 4, 2
NT = (((1,), (1,)), ((), ()))
MIB = 1 << 20
FREE = pl.CostEstimate(flops=0, bytes_accessed=0, transcendentals=0)


def device(x, y, z, core):
    return (((x % NX) * NZL + z % NZL) * (NY * NZH) + (y % NY) * NZH + (z // NZL) % NZH) * 2 + core


def pairs(move):
    out = []
    for x in range(NX):
        for y in range(NY):
            for z in range(NZL * NZH):
                for core in range(2):
                    out.append((device(x, y, z, core), device(*move(x, y, z, core))))
    return out


def send(value, name, dx=0, dy=0, dz=0, dzl=0, dcore=0, split=0):
    def move(x, y, z, core):
        low = z // NZL * NZL + (z % NZL + dzl) % NZL + (2 * core - 1) * split
        return x + dx, y + dy, (low + dz) % (NZL * NZH), core ^ dcore

    with jax.named_scope(name):
        return lax.ppermute(value, AXES, pairs(move))


LONG = pl.CostEstimate(flops=4000000000, bytes_accessed=0, transcendentals=0)


def pass_kernel(pos_ref, _, out_ref):
    for i in range(out_ref.shape[0]):
        out_ref[i] = pos_ref[i]


def pass_on(pos, held):
    return pl.pallas_call(
        pass_kernel,
        in_specs=[scalars(), anywhere()],
        out_specs=scalars(),
        out_shape=jax.ShapeDtypeStruct(pos.shape, pos.dtype),
        compiler_params=pltpu.CompilerParams(vmem_limit_bytes=MIB),
        cost_estimate=LONG,
        name="pass",
    )(pos, held)


def after(value, *others):
    return lax.optimization_barrier((value, *others))


def whole():
    return pl.BlockSpec(memory_space=pltpu.VMEM)


def anywhere():
    return pl.BlockSpec(memory_space=pl.ANY)


def scalars():
    return pl.BlockSpec(memory_space=pltpu.SMEM)


def move_all(moves, sems):
    copies = [pltpu.make_async_copy(source, target, sems.at[i]) for i, (source, target) in enumerate(moves)]
    for copy in copies:
        copy.start()
    for copy in copies:
        copy.wait()


def form_block(acts_ref, backs_ref, outs, prod_ref):
    count, layers, width, toks = acts_ref.shape
    scale = toks ** (-0.5)
    row = lax.broadcasted_iota(jnp.int32, (count, 128), 0) % 4
    lane = lax.broadcasted_iota(jnp.int32, (count, 128), 1) // width
    turn = (lane - row + 4) % 4
    for layer in range(layers):
        for part in range(count // 4):
            rows = pl.ds(part * 4, 4)
            left = backs_ref[rows, layer].reshape(4 * width, toks)
            right = acts_ref[rows, layer].reshape(4 * width, toks)
            prod_ref[layer, pl.ds(part * 128, 128), :] = lax.dot_general(
                left, right, NT, preferred_element_type=jnp.float32
            )
        for group in range(width // 4):
            held = [prod_ref[layer, pl.ds(group * 4 + s, count, stride=width), :] for s in range(4)]
            half = [jnp.where(row % 2 == 1, held[(r + 1) % 4], held[r]) for r in range(4)]
            full = [jnp.where(row >= 2, half[(r + 2) % 4], half[r]) for r in range(4)]
            full = [full[0]] + [pltpu.roll(full[r], r * width, 1) for r in range(1, 4)]
            low = jnp.where(turn == 1, full[1], full[0])
            high = jnp.where(turn == 3, full[3], full[2])
            tile = jnp.where(turn >= 2, high, low)
            at = layer * width * width + group * 128
            value = (tile * scale).astype(outs[0].dtype)
            for out_ref in outs:
                out_ref[:, pl.ds(at, 128)] = value


def form_kernel(block, acts_hbm, backs_hbm, *refs):
    outs, (acts_ref, backs_ref, prod_ref, sems) = refs[:-4], refs[-4:]
    steps = acts_hbm.shape[0] // block

    def fetch(i):
        rows = pl.ds(pl.multiple_of(i * block, block), block)
        return (
            pltpu.make_async_copy(acts_hbm.at[rows], acts_ref.at[rows], sems.at[0, i]),
            pltpu.make_async_copy(backs_hbm.at[rows], backs_ref.at[rows], sems.at[1, i]),
        )

    for i in range(steps):
        for copy in fetch(i):
            copy.start()

    for cut, half_ref in enumerate(outs[1:] or (None,)):
        first = cut * steps // max(len(outs) - 1, 1)

        def step(i, carry):
            rows = pl.ds(pl.multiple_of(i * block, block), block)
            here = pl.ds(pl.multiple_of((i - first) * block, block), block)
            for copy in fetch(i):
                copy.wait()
            targets = [outs[0].at[rows]] + ([] if half_ref is None else [half_ref.at[here]])
            form_block(acts_ref.at[rows], backs_ref.at[rows], targets, prod_ref)
            return carry

        lax.fori_loop(first, first + steps // max(len(outs) - 1, 1), step, 0)


def form_grads(acts, backs, cuts=0, block=32):
    count, layers, width, toks = acts.shape
    entries = layers * width * width
    shapes = [jax.ShapeDtypeStruct((rows, entries), jnp.bfloat16) for rows in [count] + [count // max(cuts, 1)] * cuts]
    return pl.pallas_call(
        functools.partial(form_kernel, block),
        in_specs=[anywhere()] * 2,
        out_specs=[whole() for _ in shapes],
        out_shape=shapes,
        scratch_shapes=[
            pltpu.VMEM(acts.shape, acts.dtype),
            pltpu.VMEM(backs.shape, backs.dtype),
            pltpu.VMEM((layers, block * width, 128), jnp.float32),
            pltpu.SemaphoreType.DMA((2, count // block)),
        ],
        compiler_params=pltpu.CompilerParams(vmem_limit_bytes=57 * MIB),
        cost_estimate=FREE,
        name="form",
    )(acts, backs)


def apply_kernel(pos_ref, *refs):
    grads, precs = refs[:NX], refs[NX : NX + NZL]
    out_ref, query_ref, rows_ref, sems = refs[NX + NZL :]
    x, zl = pos_ref[0], pos_ref[1]
    moves = []
    for s in range(NX):
        count = grads[s].shape[0]
        at = pl.multiple_of(lax.rem(x + s, NX) * count, count)
        moves.append((grads[s], query_ref.at[pl.ds(at, count)]))
    for s in range(NZL):
        count = precs[s].shape[1]
        at = pl.multiple_of(lax.rem(zl + s, NZL) * count, count)
        moves.append((precs[s], rows_ref.at[:, pl.ds(at, count)]))
    move_all(moves, sems)
    layers, rows, grad = rows_ref.shape
    for layer in range(layers):
        prod = lax.dot_general(
            query_ref[:, layer * grad : (layer + 1) * grad],
            rows_ref[layer],
            NT,
            preferred_element_type=jnp.float32,
        )
        out_ref[:, layer * rows : (layer + 1) * rows] = prod.astype(out_ref.dtype)


def apply_rows(pos, grads, precs):
    count, entries = grads[0].shape
    layers, rows, grad = precs[0].shape
    return pl.pallas_call(
        apply_kernel,
        in_specs=[scalars()] + [whole()] * (NX + NZL),
        out_specs=whole(),
        out_shape=jax.ShapeDtypeStruct((NX * count, layers * NZL * rows), jnp.bfloat16),
        scratch_shapes=[
            pltpu.VMEM((NX * count, entries), jnp.bfloat16),
            pltpu.VMEM((layers, NZL * rows, grad), jnp.bfloat16),
            pltpu.SemaphoreType.DMA((NX + NZL,)),
        ],
        compiler_params=pltpu.CompilerParams(vmem_limit_bytes=16 * MIB),
        cost_estimate=FREE,
        name="apply",
    )(pos, *grads, *precs)


def join_kernel(pos_ref, *refs):
    parts, (out_ref, sems) = refs[:NZL], refs[NZL:]
    zl = pos_ref[1]
    count = parts[0].shape[0] // NX
    moves = []
    for s in range(NZL):
        at = pl.multiple_of(lax.rem(zl + s, NZL) * count, count)
        for x in range(NX):
            moves.append((parts[s].at[pl.ds(x * count, count)], out_ref.at[x, pl.ds(at, count)]))
    move_all(moves, sems)


def join_queries(pos, parts):
    count, width = parts[0].shape
    out = pl.pallas_call(
        join_kernel,
        in_specs=[scalars()] + [whole()] * NZL,
        out_specs=whole(),
        out_shape=jax.ShapeDtypeStruct((NX, NZL * count // NX, width), jnp.bfloat16),
        scratch_shapes=[pltpu.SemaphoreType.DMA((NZL * NX,))],
        compiler_params=pltpu.CompilerParams(vmem_limit_bytes=16 * MIB),
        cost_estimate=pl.CostEstimate(flops=20 * 10**9, bytes_accessed=0, transcendentals=0),
        name="join",
    )(pos, *parts)
    return out.reshape(NZL * count, width)


def dot_terms(scale, left_ref, right_ref, out_ref):
    prod = lax.dot_general(left_ref[...], right_ref[...], NT, preferred_element_type=jnp.float32)
    out_ref[...] = (prod * scale).astype(out_ref.dtype)


def place_trains(y, trains, left_ref, first=0):
    count = trains[0].shape[0]
    moves = []
    for s in range(NY):
        at = pl.multiple_of(first + lax.rem(y + s, NY) * count, count)
        moves.append((trains[s], left_ref.at[pl.ds(at, count)]))
    return moves


def near_kernel(scale, pos_ref, *refs):
    queries, trains, firsts = refs[:NX], refs[NX : NX + NY], refs[NX + NY : NX + 2 * NY]
    out_ref, right_ref, left_ref, sems = refs[NX + 2 * NY :]
    x, y = pos_ref[0], pos_ref[2]
    layers = 2
    rows = queries[0].shape[1] // layers
    moves = place_trains(y, trains, left_ref) + place_trains(y, firsts, left_ref, NY * trains[0].shape[0])
    for s in range(NX):
        for layer in range(layers):
            at = pl.multiple_of(layer * NX * rows + lax.rem(x + s, NX) * rows, rows)
            moves.append((queries[s].at[:, pl.ds(layer * rows, rows)], right_ref.at[:, pl.ds(at, rows)]))
    move_all(moves, sems)
    dot_terms(scale, left_ref, right_ref, out_ref)


def score_near(pos, queries, trains, firsts, scale):
    count, entries = trains[0].shape
    total = NY * (count + firsts[0].shape[0])
    columns = queries[0].shape[0]
    return pl.pallas_call(
        functools.partial(near_kernel, scale),
        in_specs=[scalars()] + [whole()] * (NX + 2 * NY),
        out_specs=[whole(), whole()],
        out_shape=[
            jax.ShapeDtypeStruct((total, columns), jnp.bfloat16),
            jax.ShapeDtypeStruct((columns, entries), jnp.bfloat16),
        ],
        scratch_shapes=[pltpu.VMEM((total, entries), jnp.bfloat16), pltpu.SemaphoreType.DMA((2 * NX + 2 * NY,))],
        compiler_params=pltpu.CompilerParams(vmem_limit_bytes=24 * MIB),
        cost_estimate=FREE,
        name="near",
    )(pos, *queries, *trains, *firsts)


def far_kernel(scale, pos_ref, right_ref, *refs):
    trains, (out_ref, left_ref, sems) = refs[:NY], refs[NY:]
    move_all(place_trains(pos_ref[2], trains, left_ref), sems)
    dot_terms(scale, left_ref, right_ref, out_ref)


def score_far(pos, packed, trains, scale):
    count, entries = trains[0].shape
    total = NY * count
    columns = packed.shape[0]
    return pl.pallas_call(
        functools.partial(far_kernel, scale),
        in_specs=[scalars()] + [whole()] * (1 + NY),
        out_specs=whole(),
        out_shape=jax.ShapeDtypeStruct((total, columns), jnp.bfloat16),
        scratch_shapes=[pltpu.VMEM((total, entries), jnp.bfloat16), pltpu.SemaphoreType.DMA((NY,))],
        compiler_params=pltpu.CompilerParams(vmem_limit_bytes=16 * MIB),
        cost_estimate=pl.CostEstimate(flops=20 * 10**9, bytes_accessed=0, transcendentals=0),
        name="far",
    )(pos, packed, *trains)


def add_kernel(sizes, places_ref, own_ref, other_ref, *refs):
    out_ref, sum_ref, sems = refs[-3:]
    copies = []
    first = 0
    for i, size in enumerate(sizes):
        rows = pl.ds(first, size)
        first += size
        sum_ref[rows, :] = own_ref[rows, :].astype(jnp.float32) + other_ref[rows, :].astype(jnp.float32)
        at = pl.multiple_of(places_ref[i] * 16, 16)
        copies.append(pltpu.make_async_copy(sum_ref.at[rows], out_ref.at[pl.ds(at, size)], sems.at[i]))
        copies[-1].start()
    for copy in copies:
        copy.wait()


def add_terms(places, sizes, own, other, total, held=None):
    columns = own.shape[1]
    extra = [] if held is None else [held]
    return pl.pallas_call(
        functools.partial(add_kernel, sizes),
        in_specs=[scalars(), whole(), whole()] + [anywhere()] * len(extra),
        out_specs=anywhere(),
        out_shape=jax.ShapeDtypeStruct((total, columns), jnp.float32),
        scratch_shapes=[pltpu.VMEM(own.shape, jnp.float32), pltpu.SemaphoreType.DMA((len(sizes),))],
        input_output_aliases={} if held is None else {3: 0},
        compiler_params=pltpu.CompilerParams(vmem_limit_bytes=16 * MIB),
        cost_estimate=FREE,
        name="add",
    )(places, own, other, *extra)


def per_device(train_acts, train_backs, query_acts, query_backs, precond):
    t, k = lax.axis_index("train"), lax.axis_index("query")
    x, zl, y, zh = t // NZL, t % NZL, k // NZH, k % NZH
    pos = jnp.stack([x, zl, y, zh]).astype(jnp.int32)
    layers = train_acts.shape[1] * lax.axis_size("layer")
    scale = (layers * train_acts.shape[2] * train_backs.shape[2]) ** (-0.5)
    total = train_acts.shape[0] * lax.axis_size("query")
    precs = [precond, send(precond, "p_up", dz=-1), send(precond, "p_far", split=2), send(precond, "p_down", dz=1)]
    (query_grad,) = form_grads(query_acts[0], query_backs[0])
    grads = [query_grad, send(query_grad, "g_up", dx=-1), send(query_grad, "g_far", dx=2), send(query_grad, "g_down", dx=1)]
    train_acts, query_grad, precs[1] = after(train_acts, query_grad, precs[1])
    train_grad, first, second = form_grads(train_acts, train_backs, 2)
    train_grad, first, second, *got = after(train_grad, first, second, *grads, *precs)
    near = [train_grad, send(train_grad, "n_up", dy=-1), None, send(train_grad, "n_down", dy=1)]
    part = apply_rows(pos, got[:NX], got[NX:])
    parts = [part] + [send(part, "low%d" % s, dzl=-s) for s in (1, 2, 3)]
    near[1], near[3] = after(near[1], near[3])
    near[2] = send(near[1], "n_two", dy=-1)
    first, second, *parts = after(first, second, *parts)
    first = send(first, "far1", dz=NZL)
    second = send(second, "far2", dz=NZL)
    mine = join_queries(pos, parts)
    queries = [mine, send(mine, "r_up", dx=-1), None, send(mine, "r_down", dx=1)]
    later = pass_on(pos, first)
    queries[1], queries[3], near[2], again, later = after(queries[1], queries[3], near[2], first, later)
    firsts = [first, send(again, "a1", dy=-1), None, send(first, "a3", dy=1)]
    queries[2] = send(queries[1], "r_next", dx=-1)
    second, firsts[1], firsts[3] = after(second, firsts[1], firsts[3])
    firsts[2] = send(firsts[3], "a2", dy=1)
    seconds = [second, send(second, "b1", dy=-1), None, send(second, "b3", dy=1)]
    seconds[2] = send(seconds[1], "b2", dy=-1)
    later, *firsts = after(later, *firsts)
    last = later
    terms, packed = score_near(last, queries, near, firsts, scale)
    other = send(terms, "swap", dcore=1)
    last_terms = score_far(pos, packed, seconds, scale)
    last_other = send(last_terms, "swap_last", dcore=1)
    count, cut, rest = near[0].shape[0], firsts[0].shape[0], seconds[0].shape[0]
    ys = jnp.arange(NY, dtype=jnp.int32) * NZH
    near_rows, far_rows = (ys + zh) * (count // 16), (ys + 1 - zh) * (count // 16)
    places = jnp.concatenate([near_rows, far_rows]).astype(jnp.int32)
    out = add_terms(places, (count,) * NY + (cut,) * NY, terms, other, total)
    places = (far_rows + cut // 16).astype(jnp.int32)
    return add_terms(places, (rest,) * NY, last_terms, last_other, total, out)


def solution(mesh):
    in_specs = (
        P(("train", "query"), "layer", None, None),
        P(("train", "query"), "layer", None, None),
        P("query", "train", "layer", None, None),
        P("query", "train", "layer", None, None),
        P("layer", "train", None),
    )
    out_specs = P("train", "query")
    return jax.shard_map(
        per_device, mesh=mesh, in_specs=in_specs, out_specs=out_specs, check_vma=False
    )
```

```python
import functools

import jax
import jax.numpy as jnp
from jax import lax
from jax.experimental import pallas as pl
from jax.experimental.pallas import tpu as pltpu
from jax.sharding import PartitionSpec as P

AXES = ("train", "query", "layer")
NX, NY, NZL, NZH = 4, 4, 4, 2
NT = (((1,), (1,)), ((), ()))
MIB = 1 << 20
FREE = pl.CostEstimate(flops=0, bytes_accessed=0, transcendentals=0)


def device(x, y, z, core):
    return (((x % NX) * NZL + z % NZL) * (NY * NZH) + (y % NY) * NZH + (z // NZL) % NZH) * 2 + core


def pairs(move):
    out = []
    for x in range(NX):
        for y in range(NY):
            for z in range(NZL * NZH):
                for core in range(2):
                    out.append((device(x, y, z, core), device(*move(x, y, z, core))))
    return out


def send(value, name, dx=0, dy=0, dz=0, dzl=0, dcore=0, split=0):
    def move(x, y, z, core):
        low = z // NZL * NZL + (z % NZL + dzl) % NZL + (2 * core - 1) * split
        return x + dx, y + dy, (low + dz) % (NZL * NZH), core ^ dcore

    with jax.named_scope(name):
        return lax.ppermute(value, AXES, pairs(move))


LONG = pl.CostEstimate(flops=4000000000, bytes_accessed=0, transcendentals=0)


def pass_on(pos, held):
    return pl.pallas_call(
        lambda pos_ref, held_ref, out_ref: None,
        in_specs=[pl.BlockSpec(memory_space=pl.ANY)] * 2,
        out_specs=pl.BlockSpec(memory_space=pl.ANY),
        out_shape=jax.ShapeDtypeStruct(pos.shape, pos.dtype),
        input_output_aliases={0: 0},
        compiler_params=pltpu.CompilerParams(vmem_limit_bytes=MIB),
        cost_estimate=LONG,
        name="pass",
    )(pos, held)


def after(value, *others):
    return lax.optimization_barrier((value, *others))


def whole():
    return pl.BlockSpec(memory_space=pltpu.VMEM)


def anywhere():
    return pl.BlockSpec(memory_space=pl.ANY)


def scalars():
    return pl.BlockSpec(memory_space=pltpu.SMEM)


def move_all(moves):
    for source, target in moves:
        target[...] = source[...]


def form_block(acts_ref, backs_ref, outs, prod_ref):
    count, layers, width, toks = acts_ref.shape
    scale = toks ** (-0.5)
    row = lax.broadcasted_iota(jnp.int32, (count, 128), 0) % 4
    lane = lax.broadcasted_iota(jnp.int32, (count, 128), 1) // width
    turn = (lane - row + 4) % 4
    for layer in range(layers):
        for part in range(count // 4):
            rows = pl.ds(part * 4, 4)
            left = backs_ref[rows, layer].reshape(4 * width, toks)
            right = acts_ref[rows, layer].reshape(4 * width, toks)
            prod_ref[layer, pl.ds(part * 128, 128), :] = lax.dot_general(
                left, right, NT, preferred_element_type=jnp.float32
            )
        for group in range(width // 4):
            held = [prod_ref[layer, pl.ds(group * 4 + s, count, stride=width), :] for s in range(4)]
            half = [jnp.where(row % 2 == 1, held[(r + 1) % 4], held[r]) for r in range(4)]
            full = [jnp.where(row >= 2, half[(r + 2) % 4], half[r]) for r in range(4)]
            full = [full[0]] + [pltpu.roll(full[r], r * width, 1) for r in range(1, 4)]
            low = jnp.where(turn == 1, full[1], full[0])
            high = jnp.where(turn == 3, full[3], full[2])
            tile = jnp.where(turn >= 2, high, low)
            at = layer * width * width + group * 128
            value = (tile * scale).astype(outs[0].dtype)
            for out_ref in outs:
                out_ref[:, pl.ds(at, 128)] = value


def form_kernel(block, acts_hbm, backs_hbm, *refs):
    outs, (acts_ref, backs_ref, prod_ref, sems) = refs[:-4], refs[-4:]
    steps = acts_hbm.shape[0] // block

    def fetch(i):
        rows = pl.ds(pl.multiple_of(i * block, block), block)
        return (
            pltpu.make_async_copy(acts_hbm.at[rows], acts_ref.at[rows], sems.at[0, i]),
            pltpu.make_async_copy(backs_hbm.at[rows], backs_ref.at[rows], sems.at[1, i]),
        )

    for i in range(steps):
        for copy in fetch(i):
            copy.start()

    for cut, half_ref in enumerate(outs[1:] or (None,)):
        first = cut * steps // max(len(outs) - 1, 1)

        def step(i, carry):
            rows = pl.ds(pl.multiple_of(i * block, block), block)
            here = pl.ds(pl.multiple_of((i - first) * block, block), block)
            for copy in fetch(i):
                copy.wait()
            targets = [outs[0].at[rows]] + ([] if half_ref is None else [half_ref.at[here]])
            form_block(acts_ref.at[rows], backs_ref.at[rows], targets, prod_ref)
            return carry

        lax.fori_loop(first, first + steps // max(len(outs) - 1, 1), step, 0)


def form_grads(acts, backs, cuts=0, block=32):
    count, layers, width, toks = acts.shape
    entries = layers * width * width
    shapes = [jax.ShapeDtypeStruct((rows, entries), jnp.bfloat16) for rows in [count] + [count // max(cuts, 1)] * cuts]
    return pl.pallas_call(
        functools.partial(form_kernel, block),
        in_specs=[anywhere()] * 2,
        out_specs=[whole() for _ in shapes],
        out_shape=shapes,
        scratch_shapes=[
            pltpu.VMEM(acts.shape, acts.dtype),
            pltpu.VMEM(backs.shape, backs.dtype),
            pltpu.VMEM((layers, block * width, 128), jnp.float32),
            pltpu.SemaphoreType.DMA((2, count // block)),
        ],
        compiler_params=pltpu.CompilerParams(vmem_limit_bytes=57 * MIB),
        cost_estimate=FREE,
        name="form",
    )(acts, backs)


def apply_kernel(pos_ref, *refs):
    grads, precs = refs[:NX], refs[NX : NX + NZL]
    out_ref, query_ref, rows_ref = refs[NX + NZL :]
    x, zl = pos_ref[0], pos_ref[1]
    moves = []
    for s in range(NX):
        count = grads[s].shape[0]
        at = pl.multiple_of(lax.rem(x + s, NX) * count, count)
        moves.append((grads[s], query_ref.at[pl.ds(at, count)]))
    for s in range(NZL):
        count = precs[s].shape[1]
        at = pl.multiple_of(lax.rem(zl + s, NZL) * count, count)
        moves.append((precs[s], rows_ref.at[:, pl.ds(at, count)]))
    move_all(moves)
    layers, rows, grad = rows_ref.shape
    for layer in range(layers):
        prod = lax.dot_general(
            query_ref[:, layer * grad : (layer + 1) * grad],
            rows_ref[layer],
            NT,
            preferred_element_type=jnp.float32,
        )
        out_ref[:, layer * rows : (layer + 1) * rows] = prod.astype(out_ref.dtype)


def apply_rows(pos, grads, precs):
    count, entries = grads[0].shape
    layers, rows, grad = precs[0].shape
    return pl.pallas_call(
        apply_kernel,
        in_specs=[scalars()] + [whole()] * (NX + NZL),
        out_specs=whole(),
        out_shape=jax.ShapeDtypeStruct((NX * count, layers * NZL * rows), jnp.bfloat16),
        scratch_shapes=[
            pltpu.VMEM((NX * count, entries), jnp.bfloat16),
            pltpu.VMEM((layers, NZL * rows, grad), jnp.bfloat16),
        ],
        compiler_params=pltpu.CompilerParams(vmem_limit_bytes=16 * MIB),
        cost_estimate=FREE,
        name="apply",
    )(pos, *grads, *precs)


def join_kernel(pos_ref, *refs):
    parts, out_ref = refs[:NZL], refs[NZL]
    zl = pos_ref[1]
    count = parts[0].shape[0] // NX
    moves = []
    for s in range(NZL):
        at = pl.multiple_of(lax.rem(zl + s, NZL) * count, count)
        for x in range(NX):
            moves.append((parts[s].at[pl.ds(x * count, count)], out_ref.at[x, pl.ds(at, count)]))
    move_all(moves)


def join_queries(pos, parts):
    count, width = parts[0].shape
    out = pl.pallas_call(
        join_kernel,
        in_specs=[scalars()] + [whole()] * NZL,
        out_specs=whole(),
        out_shape=jax.ShapeDtypeStruct((NX, NZL * count // NX, width), jnp.bfloat16),
        compiler_params=pltpu.CompilerParams(vmem_limit_bytes=16 * MIB),
        cost_estimate=pl.CostEstimate(flops=20 * 10**9, bytes_accessed=0, transcendentals=0),
        name="join",
    )(pos, *parts)
    return out.reshape(NZL * count, width)


def dot_terms(scale, left_ref, right_ref, out_ref):
    prod = lax.dot_general(left_ref[...], right_ref[...], NT, preferred_element_type=jnp.float32)
    out_ref[...] = (prod * scale).astype(out_ref.dtype)


def place_trains(y, trains, left_ref, first=0):
    count = trains[0].shape[0]
    moves = []
    for s in range(NY):
        at = pl.multiple_of(first + lax.rem(y + s, NY) * count, count)
        moves.append((trains[s], left_ref.at[pl.ds(at, count)]))
    return moves


def near_kernel(scale, pos_ref, *refs):
    queries, trains, firsts = refs[:NX], refs[NX : NX + NY], refs[NX + NY : NX + 2 * NY]
    out_ref, right_ref, left_ref = refs[NX + 2 * NY :]
    x, y = pos_ref[0], pos_ref[2]
    layers = 2
    rows = queries[0].shape[1] // layers
    moves = place_trains(y, trains, left_ref) + place_trains(y, firsts, left_ref, NY * trains[0].shape[0])
    for s in range(NX):
        for layer in range(layers):
            at = pl.multiple_of(layer * NX * rows + lax.rem(x + s, NX) * rows, rows)
            moves.append((queries[s].at[:, pl.ds(layer * rows, rows)], right_ref.at[:, pl.ds(at, rows)]))
    move_all(moves)
    dot_terms(scale, left_ref, right_ref, out_ref)


def score_near(pos, queries, trains, firsts, scale):
    count, entries = trains[0].shape
    total = NY * (count + firsts[0].shape[0])
    columns = queries[0].shape[0]
    return pl.pallas_call(
        functools.partial(near_kernel, scale),
        in_specs=[scalars()] + [whole()] * (NX + 2 * NY),
        out_specs=[whole(), whole()],
        out_shape=[
            jax.ShapeDtypeStruct((total, columns), jnp.bfloat16),
            jax.ShapeDtypeStruct((columns, entries), jnp.bfloat16),
        ],
        scratch_shapes=[pltpu.VMEM((total, entries), jnp.bfloat16)],
        compiler_params=pltpu.CompilerParams(vmem_limit_bytes=24 * MIB),
        cost_estimate=FREE,
        name="near",
    )(pos, *queries, *trains, *firsts)


def far_kernel(scale, pos_ref, right_ref, *refs):
    trains, (out_ref, left_ref) = refs[:NY], refs[NY:]
    move_all(place_trains(pos_ref[2], trains, left_ref))
    dot_terms(scale, left_ref, right_ref, out_ref)


def score_far(pos, packed, trains, scale):
    count, entries = trains[0].shape
    total = NY * count
    columns = packed.shape[0]
    return pl.pallas_call(
        functools.partial(far_kernel, scale),
        in_specs=[scalars()] + [whole()] * (1 + NY),
        out_specs=whole(),
        out_shape=jax.ShapeDtypeStruct((total, columns), jnp.bfloat16),
        scratch_shapes=[pltpu.VMEM((total, entries), jnp.bfloat16)],
        compiler_params=pltpu.CompilerParams(vmem_limit_bytes=16 * MIB),
        cost_estimate=pl.CostEstimate(flops=20 * 10**9, bytes_accessed=0, transcendentals=0),
        name="far",
    )(pos, packed, *trains)


def add_kernel(sizes, places_ref, own_ref, other_ref, *refs):
    out_ref, sum_ref, sems = refs[-3:]
    copies = []
    first = 0
    for i, size in enumerate(sizes):
        rows = pl.ds(first, size)
        first += size
        sum_ref[rows, :] = own_ref[rows, :].astype(jnp.float32) + other_ref[rows, :].astype(jnp.float32)
        at = pl.multiple_of(places_ref[i] * 16, 16)
        copies.append(pltpu.make_async_copy(sum_ref.at[rows], out_ref.at[pl.ds(at, size)], sems.at[i]))
        copies[-1].start()
    for copy in copies:
        copy.wait()


def add_terms(places, sizes, own, other, total, held=None):
    columns = own.shape[1]
    extra = [] if held is None else [held]
    return pl.pallas_call(
        functools.partial(add_kernel, sizes),
        in_specs=[scalars(), whole(), whole()] + [anywhere()] * len(extra),
        out_specs=anywhere(),
        out_shape=jax.ShapeDtypeStruct((total, columns), jnp.float32),
        scratch_shapes=[pltpu.VMEM(own.shape, jnp.float32), pltpu.SemaphoreType.DMA((len(sizes),))],
        input_output_aliases={} if held is None else {3: 0},
        compiler_params=pltpu.CompilerParams(vmem_limit_bytes=16 * MIB),
        cost_estimate=FREE,
        name="add",
    )(places, own, other, *extra)


def per_device(train_acts, train_backs, query_acts, query_backs, precond):
    t, k = lax.axis_index("train"), lax.axis_index("query")
    x, zl, y, zh = t // NZL, t % NZL, k // NZH, k % NZH
    pos = jnp.stack([x, zl, y, zh]).astype(jnp.int32)
    layers = train_acts.shape[1] * lax.axis_size("layer")
    scale = (layers * train_acts.shape[2] * train_backs.shape[2]) ** (-0.5)
    total = train_acts.shape[0] * lax.axis_size("query")
    precs = [precond, send(precond, "p_up", dz=-1), send(precond, "p_far", split=2), send(precond, "p_down", dz=1)]
    (query_grad,) = form_grads(query_acts[0], query_backs[0])
    grads = [query_grad, send(query_grad, "g_up", dx=-1), send(query_grad, "g_far", dx=2), send(query_grad, "g_down", dx=1)]
    train_acts, query_grad, precs[1] = after(train_acts, query_grad, precs[1])
    train_grad, first, second = form_grads(train_acts, train_backs, 2)
    train_grad, first, second, *got = after(train_grad, first, second, *grads, *precs)
    near = [train_grad, send(train_grad, "n_up", dy=-1), None, send(train_grad, "n_down", dy=1)]
    part = apply_rows(pos, got[:NX], got[NX:])
    parts = [part] + [send(part, "low%d" % s, dzl=-s) for s in (1, 2, 3)]
    near[1], near[3] = after(near[1], near[3])
    near[2] = send(near[1], "n_two", dy=-1)
    first, second, *parts = after(first, second, *parts)
    first = send(first, "far1", dz=NZL)
    second = send(second, "far2", dz=NZL)
    mine = join_queries(pos, parts)
    queries = [mine, send(mine, "r_up", dx=-1), None, send(mine, "r_down", dx=1)]
    later = pass_on(jnp.stack([x, zl, y]).astype(jnp.int32), first)
    queries[1], queries[3], near[2], again, later = after(queries[1], queries[3], near[2], first, later)
    firsts = [first, send(again, "a1", dy=-1), None, send(first, "a3", dy=1)]
    queries[2] = send(queries[1], "r_next", dx=-1)
    second, firsts[1], firsts[3] = after(second, firsts[1], firsts[3])
    firsts[2] = send(firsts[3], "a2", dy=1)
    seconds = [second, send(second, "b1", dy=-1), None, send(second, "b3", dy=1)]
    seconds[2] = send(seconds[1], "b2", dy=-1)
    later, *firsts = after(later, *firsts)
    last = later
    terms, packed = score_near(last, queries, near, firsts, scale)
    other = send(terms, "swap", dcore=1)
    last_terms = score_far(pos, packed, seconds, scale)
    last_other = send(last_terms, "swap_last", dcore=1)
    count, cut, rest = near[0].shape[0], firsts[0].shape[0], seconds[0].shape[0]
    ys = jnp.arange(NY, dtype=jnp.int32) * NZH
    near_rows, far_rows = (ys + zh) * (count // 16), (ys + 1 - zh) * (count // 16)
    places = jnp.concatenate([near_rows, far_rows]).astype(jnp.int32)
    out = add_terms(places, (count,) * NY + (cut,) * NY, terms, other, total)
    places = (far_rows + cut // 16).astype(jnp.int32)
    return add_terms(places, (rest,) * NY, last_terms, last_other, total, out)


def solution(mesh):
    in_specs = (
        P(("train", "query"), "layer", None, None),
        P(("train", "query"), "layer", None, None),
        P("query", "train", "layer", None, None),
        P("query", "train", "layer", None, None),
        P("layer", "train", None),
    )
    out_specs = P("train", "query")
    return jax.shard_map(
        per_device, mesh=mesh, in_specs=in_specs, out_specs=out_specs, check_vma=False
    )
```

```python
import functools

import jax
import jax.numpy as jnp
from jax import lax
from jax.experimental import pallas as pl
from jax.experimental.pallas import tpu as pltpu
from jax.sharding import PartitionSpec as P

AXES = ("train", "query", "layer")
NX, NY, NZL, NZH = 4, 4, 4, 2
NT = (((1,), (1,)), ((), ()))
MIB = 1 << 20
LOW_ORDER = (0, 2, 1, 3)
FREE = pl.CostEstimate(flops=0, bytes_accessed=0, transcendentals=0)


def device(x, y, z, core):
    return (((x % NX) * NZL + z % NZL) * (NY * NZH) + (y % NY) * NZH + (z // NZL) % NZH) * 2 + core


def pairs(move):
    out = []
    for x in range(NX):
        for y in range(NY):
            for z in range(NZL * NZH):
                for core in range(2):
                    out.append((device(x, y, z, core), device(*move(x, y, z, core))))
    return out


def send(value, name, dx=0, dy=0, dz=0, dzl=0, dcore=0, split=0):
    def move(x, y, z, core):
        low = z // NZL * NZL + (z % NZL + dzl) % NZL + (2 * core - 1) * split
        return x + dx, y + dy, (low + dz) % (NZL * NZH), core ^ dcore

    with jax.named_scope(name):
        return lax.ppermute(value, AXES, pairs(move))


LONG = pl.CostEstimate(flops=4000000000, bytes_accessed=0, transcendentals=0)


def pass_on(pos, held):
    return pl.pallas_call(
        lambda pos_ref, held_ref, out_ref: None,
        in_specs=[pl.BlockSpec(memory_space=pl.ANY)] * 2,
        out_specs=pl.BlockSpec(memory_space=pl.ANY),
        out_shape=jax.ShapeDtypeStruct(pos.shape, pos.dtype),
        input_output_aliases={0: 0},
        compiler_params=pltpu.CompilerParams(vmem_limit_bytes=MIB),
        cost_estimate=LONG,
        name="pass",
    )(pos, held)


def after(value, *others):
    return lax.optimization_barrier((value, *others))


def whole():
    return pl.BlockSpec(memory_space=pltpu.VMEM)


def anywhere():
    return pl.BlockSpec(memory_space=pl.ANY)


def scalars():
    return pl.BlockSpec(memory_space=pltpu.SMEM)


def move_all(moves):
    for source, target in moves:
        target[...] = source[...]


def form_block(acts_ref, backs_ref, outs, prod_ref):
    count, layers, width, toks = acts_ref.shape
    scale = toks ** (-0.5)
    row = lax.broadcasted_iota(jnp.int32, (count, 128), 0) % 4
    lane = lax.broadcasted_iota(jnp.int32, (count, 128), 1) // width
    turn = (lane - row + 4) % 4
    for layer in range(layers):
        for part in range(count // 4):
            rows = pl.ds(part * 4, 4)
            left = backs_ref[rows, layer].reshape(4 * width, toks)
            right = acts_ref[rows, layer].reshape(4 * width, toks)
            prod_ref[layer, pl.ds(part * 128, 128), :] = lax.dot_general(
                left, right, NT, preferred_element_type=jnp.float32
            )
        for group in range(width // 4):
            held = [prod_ref[layer, pl.ds(group * 4 + s, count, stride=width), :] for s in range(4)]
            half = [jnp.where(row % 2 == 1, held[(r + 1) % 4], held[r]) for r in range(4)]
            full = [jnp.where(row >= 2, half[(r + 2) % 4], half[r]) for r in range(4)]
            full = [full[0]] + [pltpu.roll(full[r], r * width, 1) for r in range(1, 4)]
            low = jnp.where(turn == 1, full[1], full[0])
            high = jnp.where(turn == 3, full[3], full[2])
            tile = jnp.where(turn >= 2, high, low)
            at = layer * width * width + group * 128
            value = (tile * scale).astype(outs[0].dtype)
            for out_ref in outs:
                out_ref[:, pl.ds(at, 128)] = value


def form_kernel(block, acts_hbm, backs_hbm, *refs):
    outs, (acts_ref, backs_ref, prod_ref, sems) = refs[:-4], refs[-4:]
    steps = acts_hbm.shape[0] // block

    def fetch(i):
        rows = pl.ds(pl.multiple_of(i * block, block), block)
        return (
            pltpu.make_async_copy(acts_hbm.at[rows], acts_ref.at[rows], sems.at[0, i]),
            pltpu.make_async_copy(backs_hbm.at[rows], backs_ref.at[rows], sems.at[1, i]),
        )

    for i in range(steps):
        for copy in fetch(i):
            copy.start()

    for cut, half_ref in enumerate(outs[1:] or (None,)):
        first = cut * steps // max(len(outs) - 1, 1)

        def step(i, carry):
            rows = pl.ds(pl.multiple_of(i * block, block), block)
            here = pl.ds(pl.multiple_of((i - first) * block, block), block)
            for copy in fetch(i):
                copy.wait()
            targets = [outs[0].at[rows]] + ([] if half_ref is None else [half_ref.at[here]])
            form_block(acts_ref.at[rows], backs_ref.at[rows], targets, prod_ref)
            return carry

        lax.fori_loop(first, first + steps // max(len(outs) - 1, 1), step, 0)


def form_grads(acts, backs, cuts=0, block=32):
    count, layers, width, toks = acts.shape
    entries = layers * width * width
    shapes = [jax.ShapeDtypeStruct((rows, entries), jnp.bfloat16) for rows in [count] + [count // max(cuts, 1)] * cuts]
    return pl.pallas_call(
        functools.partial(form_kernel, block),
        in_specs=[anywhere()] * 2,
        out_specs=[whole() for _ in shapes],
        out_shape=shapes,
        scratch_shapes=[
            pltpu.VMEM(acts.shape, acts.dtype),
            pltpu.VMEM(backs.shape, backs.dtype),
            pltpu.VMEM((layers, block * width, 128), jnp.float32),
            pltpu.SemaphoreType.DMA((2, count // block)),
        ],
        compiler_params=pltpu.CompilerParams(vmem_limit_bytes=57 * MIB),
        cost_estimate=FREE,
        name="form",
    )(acts, backs)


def apply_kernel(pos_ref, *refs):
    grads, precs = refs[:NX], refs[NX : NX + NZL]
    out_ref, query_ref, rows_ref = refs[NX + NZL :]
    x, zl = pos_ref[0], pos_ref[1]
    moves = []
    for s in range(NX):
        count = grads[s].shape[0]
        at = pl.multiple_of(lax.rem(x + s, NX) * count, count)
        moves.append((grads[s], query_ref.at[pl.ds(at, count)]))
    for s in range(NZL):
        count = precs[s].shape[1]
        at = pl.multiple_of(lax.rem(zl + s, NZL) * count, count)
        moves.append((precs[s], rows_ref.at[:, pl.ds(at, count)]))
    move_all(moves)
    layers, rows, grad = rows_ref.shape
    for layer in range(layers):
        prod = lax.dot_general(
            query_ref[:, layer * grad : (layer + 1) * grad],
            rows_ref[layer],
            NT,
            preferred_element_type=jnp.float32,
        )
        out_ref[:, layer * rows : (layer + 1) * rows] = prod.astype(out_ref.dtype)


def apply_rows(pos, grads, precs):
    count, entries = grads[0].shape
    layers, rows, grad = precs[0].shape
    return pl.pallas_call(
        apply_kernel,
        in_specs=[scalars()] + [whole()] * (NX + NZL),
        out_specs=whole(),
        out_shape=jax.ShapeDtypeStruct((NX * count, layers * NZL * rows), jnp.bfloat16),
        scratch_shapes=[
            pltpu.VMEM((NX * count, entries), jnp.bfloat16),
            pltpu.VMEM((layers, NZL * rows, grad), jnp.bfloat16),
        ],
        compiler_params=pltpu.CompilerParams(vmem_limit_bytes=16 * MIB),
        cost_estimate=FREE,
        name="apply",
    )(pos, *grads, *precs)


def join_kernel(pos_ref, *refs):
    parts, out_ref = refs[:NZL], refs[NZL]
    zl = pos_ref[1]
    count = parts[0].shape[0] // NX
    moves = []
    for s, shift in enumerate(LOW_ORDER):
        at = pl.multiple_of(lax.rem(zl + shift, NZL) * count, count)
        for x in range(NX):
            moves.append((parts[s].at[pl.ds(x * count, count)], out_ref.at[x, pl.ds(at, count)]))
    move_all(moves)


def join_queries(pos, parts):
    count, width = parts[0].shape
    out = pl.pallas_call(
        join_kernel,
        in_specs=[scalars()] + [whole()] * NZL,
        out_specs=whole(),
        out_shape=jax.ShapeDtypeStruct((NX, NZL * count // NX, width), jnp.bfloat16),
        compiler_params=pltpu.CompilerParams(vmem_limit_bytes=16 * MIB),
        cost_estimate=pl.CostEstimate(flops=20 * 10**9, bytes_accessed=0, transcendentals=0),
        name="join",
    )(pos, *parts)
    return out.reshape(NZL * count, width)


def dot_terms(scale, left_ref, right_ref, out_ref):
    prod = lax.dot_general(left_ref[...], right_ref[...], NT, preferred_element_type=jnp.float32)
    out_ref[...] = (prod * scale).astype(out_ref.dtype)


def place_trains(y, trains, left_ref, first=0):
    count = trains[0].shape[0]
    moves = []
    for s in range(NY):
        at = pl.multiple_of(first + lax.rem(y + s, NY) * count, count)
        moves.append((trains[s], left_ref.at[pl.ds(at, count)]))
    return moves


def near_kernel(scale, pos_ref, *refs):
    queries, trains, firsts = refs[:NX], refs[NX : NX + NY], refs[NX + NY : NX + 2 * NY]
    out_ref, right_ref, left_ref = refs[NX + 2 * NY :]
    x, y = pos_ref[0], pos_ref[2]
    layers = 2
    rows = queries[0].shape[1] // layers
    moves = place_trains(y, trains, left_ref) + place_trains(y, firsts, left_ref, NY * trains[0].shape[0])
    for s in range(NX):
        for layer in range(layers):
            at = pl.multiple_of(layer * NX * rows + lax.rem(x + s, NX) * rows, rows)
            moves.append((queries[s].at[:, pl.ds(layer * rows, rows)], right_ref.at[:, pl.ds(at, rows)]))
    move_all(moves)
    dot_terms(scale, left_ref, right_ref, out_ref)


def score_near(pos, queries, trains, firsts, scale):
    count, entries = trains[0].shape
    total = NY * (count + firsts[0].shape[0])
    columns = queries[0].shape[0]
    return pl.pallas_call(
        functools.partial(near_kernel, scale),
        in_specs=[scalars()] + [whole()] * (NX + 2 * NY),
        out_specs=[whole(), whole()],
        out_shape=[
            jax.ShapeDtypeStruct((total, columns), jnp.bfloat16),
            jax.ShapeDtypeStruct((columns, entries), jnp.bfloat16),
        ],
        scratch_shapes=[pltpu.VMEM((total, entries), jnp.bfloat16)],
        compiler_params=pltpu.CompilerParams(vmem_limit_bytes=24 * MIB),
        cost_estimate=FREE,
        name="near",
    )(pos, *queries, *trains, *firsts)


def far_kernel(scale, pos_ref, right_ref, *refs):
    trains, (out_ref, left_ref) = refs[:NY], refs[NY:]
    move_all(place_trains(pos_ref[2], trains, left_ref))
    dot_terms(scale, left_ref, right_ref, out_ref)


def score_far(pos, packed, trains, scale):
    count, entries = trains[0].shape
    total = NY * count
    columns = packed.shape[0]
    return pl.pallas_call(
        functools.partial(far_kernel, scale),
        in_specs=[scalars()] + [whole()] * (1 + NY),
        out_specs=whole(),
        out_shape=jax.ShapeDtypeStruct((total, columns), jnp.bfloat16),
        scratch_shapes=[pltpu.VMEM((total, entries), jnp.bfloat16)],
        compiler_params=pltpu.CompilerParams(vmem_limit_bytes=16 * MIB),
        cost_estimate=pl.CostEstimate(flops=20 * 10**9, bytes_accessed=0, transcendentals=0),
        name="far",
    )(pos, packed, *trains)


def add_kernel(sizes, places_ref, own_ref, other_ref, *refs):
    out_ref, sum_ref, sems = refs[-3:]
    copies = []
    first = 0
    for i, size in enumerate(sizes):
        rows = pl.ds(first, size)
        first += size
        sum_ref[rows, :] = own_ref[rows, :].astype(jnp.float32) + other_ref[rows, :].astype(jnp.float32)
        at = pl.multiple_of(places_ref[i] * 16, 16)
        copies.append(pltpu.make_async_copy(sum_ref.at[rows], out_ref.at[pl.ds(at, size)], sems.at[i]))
        copies[-1].start()
    for copy in copies:
        copy.wait()


def add_terms(places, sizes, own, other, total, held=None):
    columns = own.shape[1]
    extra = [] if held is None else [held]
    return pl.pallas_call(
        functools.partial(add_kernel, sizes),
        in_specs=[scalars(), whole(), whole()] + [anywhere()] * len(extra),
        out_specs=anywhere(),
        out_shape=jax.ShapeDtypeStruct((total, columns), jnp.float32),
        scratch_shapes=[pltpu.VMEM(own.shape, jnp.float32), pltpu.SemaphoreType.DMA((len(sizes),))],
        input_output_aliases={} if held is None else {3: 0},
        compiler_params=pltpu.CompilerParams(vmem_limit_bytes=16 * MIB),
        cost_estimate=FREE,
        name="add",
    )(places, own, other, *extra)


def per_device(train_acts, train_backs, query_acts, query_backs, precond):
    t, k = lax.axis_index("train"), lax.axis_index("query")
    x, zl, y, zh = t // NZL, t % NZL, k // NZH, k % NZH
    pos = jnp.stack([x, zl, y, zh]).astype(jnp.int32)
    layers = train_acts.shape[1] * lax.axis_size("layer")
    scale = (layers * train_acts.shape[2] * train_backs.shape[2]) ** (-0.5)
    total = train_acts.shape[0] * lax.axis_size("query")
    precs = [precond, send(precond, "p_up", dz=-1), send(precond, "p_far", split=2), send(precond, "p_down", dz=1)]
    (query_grad,) = form_grads(query_acts[0], query_backs[0])
    grads = [query_grad, send(query_grad, "g_up", dx=-1), send(query_grad, "g_far", dx=2), send(query_grad, "g_down", dx=1)]
    train_acts, query_grad, precs[1] = after(train_acts, query_grad, precs[1])
    train_grad, first, second = form_grads(train_acts, train_backs, 2)
    train_grad, first, second, *got = after(train_grad, first, second, *grads, *precs)
    near = [train_grad, send(train_grad, "n_up", dy=-1), None, send(train_grad, "n_down", dy=1)]
    part = apply_rows(pos, got[:NX], got[NX:])
    parts = [part] + [send(part, "low%d" % s, dzl=-s) for s in LOW_ORDER[1:]]
    near[1], near[3] = after(near[1], near[3])
    near[2] = send(near[1], "n_two", dy=-1)
    first, second, *parts = after(first, second, *parts)
    first = send(first, "far1", dz=NZL)
    second = send(second, "far2", dz=NZL)
    mine = join_queries(pos, parts)
    queries = [mine, send(mine, "r_up", dx=-1), None, send(mine, "r_down", dx=1)]
    later = pass_on(jnp.stack([x, zl, y]).astype(jnp.int32), first)
    queries[1], queries[3], near[2], again, later = after(queries[1], queries[3], near[2], first, later)
    firsts = [first, send(again, "a1", dy=-1), None, send(first, "a3", dy=1)]
    queries[2] = send(queries[1], "r_next", dx=-1)
    second, firsts[1], firsts[3] = after(second, firsts[1], firsts[3])
    firsts[2] = send(firsts[3], "a2", dy=1)
    seconds = [second, send(second, "b1", dy=-1), None, send(second, "b3", dy=1)]
    seconds[2] = send(seconds[1], "b2", dy=-1)
    later, *firsts = after(later, *firsts)
    last = later
    terms, packed = score_near(last, queries, near, firsts, scale)
    other = send(terms, "swap", dcore=1)
    last_terms = score_far(pos, packed, seconds, scale)
    last_other = send(last_terms, "swap_last", dcore=1)
    count, cut, rest = near[0].shape[0], firsts[0].shape[0], seconds[0].shape[0]
    ys = jnp.arange(NY, dtype=jnp.int32) * NZH
    near_rows, far_rows = (ys + zh) * (count // 16), (ys + 1 - zh) * (count // 16)
    places = jnp.concatenate([near_rows, far_rows]).astype(jnp.int32)
    out = add_terms(places, (count,) * NY + (cut,) * NY, terms, other, total)
    places = (far_rows + cut // 16).astype(jnp.int32)
    return add_terms(places, (rest,) * NY, last_terms, last_other, total, out)


def solution(mesh):
    in_specs = (
        P(("train", "query"), "layer", None, None),
        P(("train", "query"), "layer", None, None),
        P("query", "train", "layer", None, None),
        P("query", "train", "layer", None, None),
        P("layer", "train", None),
    )
    out_specs = P("train", "query")
    return jax.shard_map(
        per_device, mesh=mesh, in_specs=in_specs, out_specs=out_specs, check_vma=False
    )
```
